256 devices in a mesh: dp: 8 (over x, core), gx: 32 (over z, y).
Axes of the slice: x: 4, y: 4, z: 8, core: 2. Of those that a mesh axis runs over, the one named last changes fastest.
Arguments:
- features: bfloat16 [16, 64, 128, 8, 128], P('dp', None, 'gx'), may hold values from -6 to 6
- labels: int32 [16, 128, 8, 128], P('dp', 'gx'), may hold values from 0 to 7
- embedding: float32 [8, 64], replicated, may hold values from -4 to 4
- weight_one: bfloat16 [3, 3, 3, 64, 64], replicated, may hold values from -0.15625 to 0.15625
- weight_two: bfloat16 [3, 3, 3, 64, 64], replicated, may hold values from -0.15625 to 0.15625
- cotangent: bfloat16 [16, 64, 128, 8, 128], P('dp', None, 'gx'), may hold values from -6 to 6
Outputs:
- output: bfloat16 [16, 64, 128, 8, 128], P('dp', None, 'gx')
- grad_one: float32 [3, 3, 3, 64, 64], replicated
- grad_two: float32 [3, 3, 3, 64, 64], replicated
The draws below stay inside these ranges and needn't reach their ends.
All inputs are finite; a program needn't handle non-finite values.
Results may differ from the reference program's by a relative error of at most 0.015.
Values may be sent and summed in bfloat16 or wider, within the bound.
A program may use at most 128 MiB of HBM per device.

```python
import jax
import jax.numpy as jnp
from jax import lax

C = 64
LABELS = 8
NZ = 8
NY = 128
SAMPLES = 16
NX = 128


def set_ends(array, own_key, low, high):
    extent = array.shape
    index_at = [jax.random.randint(jax.random.fold_in(own_key, axis), (), 0, extent[axis]) for axis in range(len(extent))]
    array = array.at[tuple(index_at)].set(low)
    longest = extent.index(max(extent))
    index_at[longest] = (index_at[longest] + 1) % extent[longest]
    return array.at[tuple(index_at)].set(high)


def block_levels(stream_key, shape, cuts, low, high):
    level = 1.0
    for axis_at, shards_of in cuts:
        heights = jax.random.uniform(jax.random.fold_in(jax.random.fold_in(stream_key, 6), axis_at), (shards_of,), jnp.float32, low / len(cuts), high / len(cuts))
        level = level * jnp.repeat(jnp.exp(heights), shape[axis_at] // shards_of).reshape((-1,) + (1,) * (len(shape) - 1 - axis_at))
    return level


def noise(key, shape, scale, bound, pieces=(), dtype=jnp.bfloat16):
    result = jax.random.normal(key, shape, jnp.float32) * scale
    if len(pieces) > 0:
        result = block_levels(key, shape, pieces, -0.22, 0.18) * result
    return jnp.clip(result, min=-bound, max=bound).astype(dtype)


def setup_inputs(seed: int = 0) -> dict:
    streams_of = jax.random.split(jax.random.key(seed), 7)
    features = noise(streams_of[0], (SAMPLES, C, NX, NZ, NY), 1.0, 6.0, ((0, 8), (2, 32)))
    labels = set_ends(jax.random.randint(streams_of[1], (SAMPLES, NX, NZ, NY), 0, LABELS), jax.random.fold_in(streams_of[1], 1), 0, LABELS - 1).astype(jnp.int32)
    embedding = noise(streams_of[2], (LABELS, C), 1.0, 4.0, (), jnp.float32)
    weight_one = noise(streams_of[3], (3, 3, 3, C, C), (27 * C) ** -0.5, 0.15625)
    weight_two = noise(streams_of[4], (3, 3, 3, C, C), (27 * C) ** -0.5, 0.15625)
    cotangent = noise(streams_of[5], (SAMPLES, C, NX, NZ, NY), 1.0, 6.0, ((0, 8), (2, 32)))
    return dict(features=features, labels=labels, embedding=embedding, weight_one=weight_one, weight_two=weight_two, cotangent=cotangent)


def periodic(field, width):
    return jnp.concatenate([field[:, :, -width:], field, field[:, :, :width]], axis=2)


def convolve(extended, kernel):
    return lax.conv_general_dilated(extended, kernel, (1, 1, 1), ((0, 0), (1, 1), (1, 1)), dimension_numbers=("NCDHW", "DHWIO", "NCDHW"), preferred_element_type=jnp.float32)


def tap_terms(extended, partner):
    padded = jnp.pad(extended, ((0, 0), (0, 0), (0, 0), (1, 1), (1, 1)))
    planes = partner.shape[2]
    depth = partner.shape[3]
    span = partner.shape[4]
    terms = []
    for first in range(3):
        for second in range(3):
            for third in range(3):
                window = padded[:, :, first:first + planes, second:second + depth, third:third + span]
                terms.append(jnp.einsum("bixzy,boxzy->io", window.astype(jnp.float32), partner.astype(jnp.float32)))
    stacked = jnp.stack(terms)
    return stacked.reshape(3, 3, 3, stacked.shape[1], stacked.shape[2])


def one_sample(items, embedding, weight_one, weight_two):
    feats, labs, cots = items
    feats = feats[None]
    labs = labs[None]
    cots = cots[None]
    looked = jnp.take(embedding, labs, axis=0)
    base = (feats.astype(jnp.float32) + jnp.moveaxis(looked, -1, 1)).astype(jnp.bfloat16)
    base_ext = periodic(base, 1)
    pre = convolve(base_ext, weight_one)
    hidden = jax.nn.silu(pre).astype(jnp.bfloat16)
    hidden_ext = periodic(hidden, 1)
    output = (base.astype(jnp.float32) + convolve(hidden_ext, weight_two)).astype(jnp.bfloat16)
    flipped = jnp.swapaxes(weight_two[::-1, ::-1, ::-1], 3, 4)
    d_hidden = convolve(periodic(cots, 1), flipped)
    sig = jax.nn.sigmoid(pre)
    d_pre = (d_hidden * sig * (1.0 + pre * (1.0 - sig))).astype(jnp.bfloat16)
    grad_two = tap_terms(hidden_ext, cots)
    grad_one = tap_terms(base_ext, d_pre)
    return output[0], grad_one, grad_two


def reference(features, labels, embedding, weight_one, weight_two, cotangent):
    outputs, ones, twos = lax.map(lambda items: one_sample(items, embedding, weight_one, weight_two), (features, labels, cotangent))
    count = features.shape[0] * features.shape[2] * features.shape[3] * features.shape[4]
    scale = 1.0 / (count ** 0.5)
    return outputs, jnp.sum(ones, axis=0) * scale, jnp.sum(twos, axis=0) * scale
```

```python
import functools
import math

import jax
import jax.numpy as jnp
from jax import lax
from jax.experimental import pallas as pl
from jax.experimental.pallas import tpu as pltpu
from jax.sharding import PartitionSpec as P

MESH = pl.DeviceIdType.MESH
F32 = jnp.float32
BF16 = jnp.bfloat16

CH = 64
PLANES = 4
DEPTH = 8
SPAN = 128
CELLS = DEPTH * SPAN
PADDED = CELLS + 2 * SPAN
TRIPLE = 3 * CH
SAMPLES = 2
PACKED = 1024
Y_RING = 4
NT = (((1,), (1,)), ((), ()))


def rows(start, size, unit=16):
    return pl.ds(pl.multiple_of(start, unit), size)


def shifted(value):
    lane = lax.broadcasted_iota(jnp.int32, value.shape, 1)
    after = jnp.where(lane == 0, 0.0, pltpu.roll(value, 1, 1))
    before = jnp.where(lane == SPAN - 1, 0.0, pltpu.roll(value, SPAN - 1, 1))
    return before, after


def body(
    dp_count,
    z_count,
    scale,
    feat_hbm,
    labels_hbm,
    emb_hbm,
    one_hbm,
    two_hbm,
    cot_hbm,
    out_hbm,
    grad_one_ref,
    grad_two_ref,
    feat,
    cot,
    labels,
    emb,
    one,
    two,
    wide,
    base3,
    cot3,
    hid3,
    dpre3,
    factor,
    part,
    w_one,
    w_two,
    w_back,
    acc,
    packed,
    got_dp,
    mine_y,
    got_y,
    all_z,
    full,
    in_sem,
    out_sem,
    halo_send,
    halo_recv,
    dp_send,
    dp_recv,
    y_send,
    y_recv,
    z_send,
    z_recv,
    yg_send,
    yg_recv,
    dg_send,
    dg_recv,
):
    me_dp = lax.axis_index("dp")
    me_gx = lax.axis_index("gx")
    gx_count = z_count * Y_RING
    me_z = me_gx // Y_RING
    me_y = me_gx % Y_RING
    left = (me_dp, (me_gx + gx_count - 1) % gx_count)
    right = (me_dp, (me_gx + 1) % gx_count)

    def dp_peer(k):
        return ((me_dp + k) % dp_count, me_gx)

    def y_peer(k):
        return (me_dp, me_z * Y_RING + (me_y + k) % Y_RING)

    def z_peer(k):
        return (me_dp, ((me_z + k) % z_count) * Y_RING + me_y)

    loads = []
    for at, (src, dst) in enumerate(
        (
            (emb_hbm, emb),
            (labels_hbm, labels),
            (feat_hbm.at[0], feat.at[0]),
            (feat_hbm.at[1], feat.at[1]),
            (cot_hbm.at[0], cot.at[0]),
            (cot_hbm.at[1], cot.at[1]),
            (one_hbm, one),
            (two_hbm, two),
        )
    ):
        copy = pltpu.make_async_copy(src, dst, in_sem.at[at])
        copy.start()
        loads.append(copy)

    for field in (base3, hid3):
        for s in range(SAMPLES):
            for plane in range(PLANES + 2):
                low = plane * TRIPLE + CH
                field[s, low : low + CH, 0:SPAN] = jnp.zeros((CH, SPAN), BF16)
                field[s, low : low + CH, PADDED - SPAN : PADDED] = jnp.zeros((CH, SPAN), BF16)
    part[:, 0:SPAN] = jnp.zeros((TRIPLE, SPAN), F32)
    part[:, PADDED - SPAN : PADDED] = jnp.zeros((TRIPLE, SPAN), F32)

    barrier = pltpu.get_barrier_semaphore()
    peers = [left, right]
    peers += [dp_peer(k) for k in range(1, dp_count)]
    peers += [y_peer(k) for k in range(1, Y_RING)]
    peers += [z_peer(k) for k in range(1, z_count)]
    for peer in peers:
        pl.semaphore_signal(barrier, inc=1, device_id=peer, device_id_type=MESH)

    eye = (
        lax.broadcasted_iota(jnp.int32, (CH, CH), 0) == lax.broadcasted_iota(jnp.int32, (CH, CH), 1)
    ).astype(BF16)
    loads[0].wait()
    loads[1].wait()
    table = emb[...]
    high = table.astype(BF16)
    rest = table - high.astype(F32)
    middle = rest.astype(BF16)
    low = (rest - middle.astype(F32)).astype(BF16)
    pieces = jnp.concatenate(
        [high.astype(F32), middle.astype(F32), low.astype(F32), jnp.zeros((8, CH), F32)], axis=0
    ).astype(BF16)
    turned = lax.dot_general(eye, pieces, NT, preferred_element_type=F32).astype(BF16)

    def widen(source, s):
        def step(c, carry):
            block = source[s, pl.ds(c * 8, 8)].reshape(8 * PLANES * DEPTH, SPAN)
            wide[s, rows(c * 8 * PLANES * DEPTH, 8 * PLANES * DEPTH), :] = block.astype(F32)
            return carry

        lax.fori_loop(0, CH // 8, step, 0)

    def put(field, s, plane, z, value, order):
        before, after = shifted(value)
        first, last = (after, before) if order > 0 else (before, after)
        low = plane * TRIPLE
        lanes = slice((z + 1) * SPAN, (z + 2) * SPAN)
        field[s, rows(low, CH), lanes] = first.astype(BF16)
        field[s, rows(low + CH, CH), lanes] = value.astype(BF16)
        field[s, rows(low + 2 * CH, CH), lanes] = last.astype(BF16)

    def base_plane(s, x):
        kind = lax.broadcasted_iota(jnp.int32, (32, SPAN), 0) % 8
        for z in range(DEPTH):
            row = labels[s, x, z : z + 1, :]
            hot = (jnp.broadcast_to(row, (32, SPAN)) == kind).astype(F32).astype(BF16)
            looked = jnp.dot(turned, hot, preferred_element_type=F32)
            own = wide[s, pl.ds(x * DEPTH + z, CH, stride=PLANES * DEPTH), :]
            put(base3, s, x + 1, z, own + looked, 1)

    def cot_plane(s, x):
        for z in range(DEPTH):
            own = wide[s, pl.ds(x * DEPTH + z, CH, stride=PLANES * DEPTH), :]
            put(cot3, s, x + 1, z, own, -1)

    def halo(field, which, s):
        inner = slice(SPAN, SPAN + CELLS)
        copies = []
        for side, (at, to, device) in enumerate(
            ((1, PLANES + 1, left), (PLANES, 0, right))
        ):
            copies.append(
                pltpu.make_async_remote_copy(
                    src_ref=field.at[s, at * TRIPLE + CH : at * TRIPLE + 2 * CH, inner],
                    dst_ref=field.at[s, to * TRIPLE + CH : to * TRIPLE + 2 * CH, inner],
                    send_sem=halo_send.at[which, s, side],
                    recv_sem=halo_recv.at[which, s, side],
                    device_id=device,
                    device_id_type=MESH,
                )
            )
        return copies

    def halo_shifts(field, s, order):
        def step(side, carry):
            plane = side * (PLANES + 1)
            for z in range(DEPTH):
                lanes = slice((z + 1) * SPAN, (z + 2) * SPAN)
                value = field[s, rows(plane * TRIPLE + CH, CH), lanes].astype(F32)
                before, after = shifted(value)
                first, last = (after, before) if order > 0 else (before, after)
                field[s, rows(plane * TRIPLE, CH), lanes] = first.astype(BF16)
                field[s, rows(plane * TRIPLE + 2 * CH, CH), lanes] = last.astype(BF16)
            return carry

        lax.fori_loop(0, 2, step, 0)

    halos = [[halo(field, which, s) for s in range(SAMPLES)] for which, field in enumerate((base3, cot3, hid3))]

    for s in range(SAMPLES):
        loads[2 + s].wait()
        widen(feat, s)

        def plane_step(x, carry, s=s):
            base_plane(s, x)
            return carry

        lax.fori_loop(0, PLANES, plane_step, 0)
        if s == 0:
            pl.semaphore_wait(barrier, len(peers))
        for copy in halos[0][s]:
            copy.start()
    for s in range(SAMPLES):
        loads[4 + s].wait()
        widen(cot, s)

        def plane_step(x, carry, s=s):
            cot_plane(s, x)
            return carry

        lax.fori_loop(0, PLANES, plane_step, 0)
        for copy in halos[1][s]:
            copy.start()

    loads[6].wait()
    loads[7].wait()
    for b in range(3):
        for source, target in ((one, w_one), (two, w_two)):
            stacked = jnp.concatenate(
                [source[(a * 3 + b) * 3 + e] for a in range(3) for e in range(3)], axis=0
            )
            target[b * CH : (b + 1) * CH, :] = lax.dot_general(
                eye, stacked, NT, preferred_element_type=F32
            ).astype(BF16)
        flat = jnp.concatenate(
            [
                lax.dot_general(
                    eye, two[((2 - a) * 3 + b) * 3 + e], NT, preferred_element_type=F32
                ).astype(BF16)
                for a in range(3)
                for e in range(3)
            ],
            axis=0,
        )
        w_back[b * CH : (b + 1) * CH, :] = lax.dot_general(
            eye, flat, NT, preferred_element_type=F32
        ).astype(BF16)

    def products(field, weights, s, x):
        part[:, SPAN : SPAN + CELLS] = jnp.dot(
            weights[...],
            field[s, rows(x * TRIPLE, 3 * TRIPLE), SPAN : SPAN + CELLS],
            preferred_element_type=F32,
        )

    def summed(z, order):
        total = part[CH : 2 * CH, (z + 1) * SPAN : (z + 2) * SPAN]
        total = total + part[0:CH, (z + 1 - order) * SPAN : (z + 2 - order) * SPAN]
        return total + part[2 * CH :, (z + 1 + order) * SPAN : (z + 2 + order) * SPAN]

    def first_layer(s, x):
        products(base3, w_one, s, x)
        for z in range(DEPTH):
            pre = summed(z, 1)
            q = jax.nn.sigmoid(pre)
            factor[s, x, :, z * SPAN : (z + 1) * SPAN] = q * (1.0 + pre * (1.0 - q))
            put(hid3, s, x + 1, z, pre * q, 1)

    def backward(s, x):
        products(cot3, w_back, s, x)
        for z in range(DEPTH):
            d_pre = summed(z, -1) * factor[s, x, :, z * SPAN : (z + 1) * SPAN]
            before, after = shifted(d_pre)
            lanes = slice(z * SPAN, (z + 1) * SPAN)
            low = x * TRIPLE
            dpre3[s, rows(low, CH), lanes] = before.astype(BF16)
            dpre3[s, rows(low + CH, CH), lanes] = d_pre.astype(BF16)
            dpre3[s, rows(low + 2 * CH, CH), lanes] = after.astype(BF16)

    def second_layer(s, x):
        products(hid3, w_two, s, x)
        for z in range(DEPTH):
            own = base3[s, rows((x + 1) * TRIPLE + CH, CH), (z + 1) * SPAN : (z + 2) * SPAN]
            wide[s, pl.ds(x * DEPTH + z, CH, stride=PLANES * DEPTH), :] = summed(z, 1) + own.astype(F32)

    def inner_planes(work):
        def step(i, carry):
            work(i // 2, 1 + i % 2)
            return carry

        lax.fori_loop(0, 4, step, 0)

    def edge_planes(work, s):
        def step(i, carry):
            work(s, 3 * i)
            return carry

        lax.fori_loop(0, 2, step, 0)

    inner_planes(first_layer)
    for s in range(SAMPLES):
        for copy in halos[0][s]:
            copy.wait_recv()
        halo_shifts(base3, s, 1)
        edge_planes(first_layer, s)
        for copy in halos[2][s]:
            copy.start()
    inner_planes(backward)
    for s in range(SAMPLES):
        for copy in halos[1][s]:
            copy.wait_recv()
        halo_shifts(cot3, s, -1)
        edge_planes(backward, s)

    def gradient(g, field, partner, partner_plane, partner_lane):
        acc[...] = jnp.zeros_like(acc)

        def step(i, carry):
            s = i // PLANES
            x = i % PLANES
            taps = jnp.concatenate(
                [
                    field[s, rows((x + a) * TRIPLE + CH, CH), b * SPAN : b * SPAN + CELLS]
                    for a in range(3)
                    for b in range(3)
                ],
                axis=0,
            )
            other = partner[
                s, rows((x + partner_plane) * TRIPLE, TRIPLE), partner_lane : partner_lane + CELLS
            ]
            acc[...] += lax.dot_general(taps, other, NT, preferred_element_type=F32)
            return carry

        lax.fori_loop(0, SAMPLES * PLANES, step, 0)
        half = 9 * CH // 2
        packed[g, 0 : 9 * CH, :] = acc[:, 0:SPAN].astype(BF16)
        packed[g, 9 * CH : 9 * CH + half, :] = jnp.concatenate(
            [acc[0:half, SPAN:TRIPLE], acc[half : 2 * half, SPAN:TRIPLE]], axis=1
        ).astype(BF16)
        packed[g, 9 * CH + half :, :] = jnp.zeros((PACKED - 9 * CH - half, SPAN), BF16)

    dp_rows = PACKED // dp_count
    y_rows = dp_rows // Y_RING

    def sum_dp(g):
        return [
            pltpu.make_async_remote_copy(
                src_ref=packed.at[g, rows(((me_dp + k) % dp_count) * dp_rows, dp_rows)],
                dst_ref=got_dp.at[g, k - 1],
                send_sem=dp_send.at[g, k - 1],
                recv_sem=dp_recv.at[g, k - 1],
                device_id=dp_peer(k),
                device_id_type=MESH,
            )
            for k in range(1, dp_count)
        ]

    def sum_y(g):
        return [
            pltpu.make_async_remote_copy(
                src_ref=mine_y.at[g, rows(((me_y + k) % Y_RING) * y_rows, y_rows)],
                dst_ref=got_y.at[g, k - 1],
                send_sem=y_send.at[g, k - 1],
                recv_sem=y_recv.at[g, k - 1],
                device_id=y_peer(k),
                device_id_type=MESH,
            )
            for k in range(1, Y_RING)
        ]

    def spread_z(g):
        return [
            pltpu.make_async_remote_copy(
                src_ref=all_z.at[g, me_z],
                dst_ref=all_z.at[g, me_z],
                send_sem=z_send.at[g, k - 1],
                recv_sem=z_recv.at[g, k - 1],
                device_id=z_peer(k),
                device_id_type=MESH,
            )
            for k in range(1, z_count)
        ]

    def my_y_rows():
        return rows(me_dp * dp_rows + me_y * y_rows, y_rows)

    def my_dp_rows():
        return rows(me_dp * dp_rows, dp_rows)

    def gather_y(g):
        return [
            pltpu.make_async_remote_copy(
                src_ref=full.at[g, my_y_rows()],
                dst_ref=full.at[g, my_y_rows()],
                send_sem=yg_send.at[g, k - 1],
                recv_sem=yg_recv.at[g, k - 1],
                device_id=y_peer(k),
                device_id_type=MESH,
            )
            for k in range(1, Y_RING)
        ]

    def gather_dp(g):
        return [
            pltpu.make_async_remote_copy(
                src_ref=full.at[g, my_dp_rows()],
                dst_ref=full.at[g, my_dp_rows()],
                send_sem=dg_send.at[g, k - 1],
                recv_sem=dg_recv.at[g, k - 1],
                device_id=dp_peer(k),
                device_id_type=MESH,
            )
            for k in range(1, dp_count)
        ]

    sent = []

    def start(copies):
        for copy in copies:
            copy.start()
        sent.extend(copies)
        return copies

    def arrived(copies):
        for copy in copies:
            copy.wait_recv()

    def stage_one(g, dp_copies):
        arrived(dp_copies)
        total = packed[g, my_dp_rows(), :].astype(F32)
        for k in range(dp_count - 1):
            total = total + got_dp[g, k].astype(F32)
        mine_y[g] = total.astype(BF16)
        return start(sum_y(g))

    def stage_two(g, y_copies):
        arrived(y_copies)
        total = mine_y[g, rows(me_y * y_rows, y_rows), :].astype(F32)
        for k in range(Y_RING - 1):
            total = total + got_y[g, k].astype(F32)
        all_z[g, me_z] = total.astype(BF16)
        return start(spread_z(g))

    def stage_three(g, z_copies):
        arrived(z_copies)
        total = all_z[g, 0].astype(F32)
        for k in range(1, z_count):
            total = total + all_z[g, k].astype(F32)
        full[g, my_y_rows(), :] = (total * scale).astype(BF16)
        return start(gather_y(g))

    def stage_four(g, yg_copies):
        arrived(yg_copies)
        return start(gather_dp(g))

    def stage_five(g, dg_copies, target):
        arrived(dg_copies)
        half = 9 * CH // 2
        for tap in range(9):
            block = full[g, tap * CH : (tap + 1) * CH, :].astype(F32)
            target[tap * 3] = block[:, 0:CH]
            target[tap * 3 + 1] = block[:, CH:]
        for piece in range(18):
            low = piece * 32
            lane = 0
            if low >= half:
                low, lane = low - half, CH
            block = full[g, 9 * CH + low : 9 * CH + low + 32, lane : lane + CH].astype(F32)
            target[(piece // 2) * 3 + 2, (piece % 2) * 32 : (piece % 2) * 32 + 32, :] = block

    gradient(0, base3, dpre3, 0, 0)
    wait_zero = start(sum_dp(0))
    for s in range(SAMPLES):
        for copy in halos[2][s]:
            copy.wait_recv()
        halo_shifts(hid3, s, 1)
    gradient(1, hid3, cot3, 1, SPAN)
    wait_one = start(sum_dp(1))
    wait_zero = stage_one(0, wait_zero)

    def two_planes(s, first):
        def step(i, carry):
            second_layer(s, first + i)
            return carry

        lax.fori_loop(0, 2, step, 0)

    def give_back(s):
        def step(c, carry):
            block = wide[s, rows(c * 8 * PLANES * DEPTH, 8 * PLANES * DEPTH), :]
            feat[s, pl.ds(c * 8, 8)] = block.reshape(8, PLANES * DEPTH, SPAN).astype(BF16)
            return carry

        lax.fori_loop(0, CH // 8, step, 0)
        copy = pltpu.make_async_copy(feat.at[s], out_hbm.at[s], out_sem.at[s])
        copy.start()
        return copy

    two_planes(0, 0)
    wait_one = stage_one(1, wait_one)
    wait_zero = stage_two(0, wait_zero)
    two_planes(0, 2)
    wait_one = stage_two(1, wait_one)
    wait_zero = stage_three(0, wait_zero)
    out_zero = give_back(0)
    two_planes(1, 0)
    wait_one = stage_three(1, wait_one)
    wait_zero = stage_four(0, wait_zero)
    two_planes(1, 2)
    wait_one = stage_four(1, wait_one)
    out_one = give_back(1)
    stage_five(0, wait_zero, grad_one_ref)
    stage_five(1, wait_one, grad_two_ref)

    out_zero.wait()
    out_one.wait()
    for field in halos:
        for side in field:
            for copy in side:
                copy.wait_send()
    for copy in sent:
        copy.wait_send()


def on_device(dp_count, z_count, features, labels, embedding, weight_one, weight_two, cotangent):
    count = SAMPLES * dp_count * PLANES * z_count * Y_RING * CELLS
    dp_rows = PACKED // dp_count
    y_rows = dp_rows // Y_RING
    flat = (SAMPLES, CH, PLANES * DEPTH, SPAN)
    dma = pltpu.SemaphoreType.DMA
    field = pltpu.VMEM((SAMPLES, (PLANES + 2) * TRIPLE, PADDED), BF16)
    output, grad_one, grad_two = pl.pallas_call(
        functools.partial(body, dp_count, z_count, 1.0 / math.sqrt(count)),
        out_shape=(
            jax.ShapeDtypeStruct(flat, BF16),
            jax.ShapeDtypeStruct((27, CH, CH), F32),
            jax.ShapeDtypeStruct((27, CH, CH), F32),
        ),
        in_specs=[pl.BlockSpec(memory_space=pl.ANY)] * 6,
        out_specs=(
            pl.BlockSpec(memory_space=pl.ANY),
            pl.BlockSpec(memory_space=pltpu.VMEM),
            pl.BlockSpec(memory_space=pltpu.VMEM),
        ),
        scratch_shapes=[
            pltpu.VMEM(flat, BF16),
            pltpu.VMEM(flat, BF16),
            pltpu.VMEM((SAMPLES, PLANES, DEPTH, SPAN), jnp.int32),
            pltpu.VMEM((8, CH), F32),
            pltpu.VMEM((27, CH, CH), BF16),
            pltpu.VMEM((27, CH, CH), BF16),
            pltpu.VMEM((SAMPLES, CH * PLANES * DEPTH, SPAN), F32),
            field,
            field,
            field,
            pltpu.VMEM((SAMPLES, PLANES * TRIPLE, CELLS), BF16),
            pltpu.VMEM((SAMPLES, PLANES, CH, CELLS), F32),
            pltpu.VMEM((TRIPLE, PADDED), F32),
            pltpu.VMEM((TRIPLE, 3 * TRIPLE), BF16),
            pltpu.VMEM((TRIPLE, 3 * TRIPLE), BF16),
            pltpu.VMEM((TRIPLE, 3 * TRIPLE), BF16),
            pltpu.VMEM((9 * CH, TRIPLE), F32),
            pltpu.VMEM((2, PACKED, SPAN), BF16),
            pltpu.VMEM((2, dp_count - 1, dp_rows, SPAN), BF16),
            pltpu.VMEM((2, dp_rows, SPAN), BF16),
            pltpu.VMEM((2, Y_RING - 1, y_rows, SPAN), BF16),
            pltpu.VMEM((2, z_count, y_rows, SPAN), BF16),
            pltpu.VMEM((2, PACKED, SPAN), BF16),
            dma((8,)),
            dma((SAMPLES,)),
            dma((3, SAMPLES, 2)),
            dma((3, SAMPLES, 2)),
            dma((2, dp_count - 1)),
            dma((2, dp_count - 1)),
            dma((2, Y_RING - 1)),
            dma((2, Y_RING - 1)),
            dma((2, max(z_count - 1, 1))),
            dma((2, max(z_count - 1, 1))),
            dma((2, Y_RING - 1)),
            dma((2, Y_RING - 1)),
            dma((2, dp_count - 1)),
            dma((2, dp_count - 1)),
        ],
        compiler_params=pltpu.CompilerParams(
            collective_id=0, has_side_effects=True, vmem_limit_bytes=56 * 1024 * 1024
        ),
        name="surrogate",
    )(
        features.reshape(flat),
        labels,
        embedding,
        weight_one.reshape(27, CH, CH),
        weight_two.reshape(27, CH, CH),
        cotangent.reshape(flat),
    )
    taps = (3, 3, 3, CH, CH)
    return output.reshape(features.shape), grad_one.reshape(taps), grad_two.reshape(taps)


def solution(mesh):
    dp_count = mesh.shape["dp"]
    z_count = mesh.shape["gx"] // Y_RING
    placed = (
        P("dp", None, "gx", None, None),
        P("dp", "gx", None, None),
        P(),
        P(),
        P(),
        P("dp", None, "gx", None, None),
    )
    return jax.shard_map(
        functools.partial(on_device, dp_count, z_count),
        mesh=mesh,
        in_specs=placed,
        out_specs=(P("dp", None, "gx", None, None), P(), P()),
        check_vma=False,
    )
```

```python
import functools
import math

import jax
import jax.numpy as jnp
from jax import lax
from jax.experimental import pallas as pl
from jax.experimental.pallas import tpu as pltpu
from jax.sharding import PartitionSpec as P

MESH = pl.DeviceIdType.MESH
F32 = jnp.float32
BF16 = jnp.bfloat16

CH = 64
PLANES = 4
DEPTH = 8
SPAN = 128
CELLS = DEPTH * SPAN
PADDED = CELLS + 2 * SPAN
TRIPLE = 3 * CH
SAMPLES = 2
PACKED = 1024
Y_RING = 4
NT = (((1,), (1,)), ((), ()))


def rows(start, size, unit=16):
    return pl.ds(pl.multiple_of(start, unit), size)


def shifted(value):
    lane = lax.broadcasted_iota(jnp.int32, value.shape, 1)
    after = jnp.where(lane == 0, 0.0, pltpu.roll(value, 1, 1))
    before = jnp.where(lane == SPAN - 1, 0.0, pltpu.roll(value, SPAN - 1, 1))
    return before, after


def body(
    dp_count,
    z_count,
    scale,
    feat_hbm,
    labels_hbm,
    emb_hbm,
    one_hbm,
    two_hbm,
    cot_hbm,
    held,
    full,
    feat,
    cot,
    labels,
    emb,
    one,
    two,
    wide,
    base3,
    cot3,
    hid3,
    dpre3,
    factor,
    part,
    w_one,
    w_two,
    w_back,
    acc,
    packed,
    got_dp,
    mine_y,
    got_y,
    all_z,
    in_sem,
    halo_send,
    halo_recv,
    dp_send,
    dp_recv,
    y_send,
    y_recv,
    z_send,
    z_recv,
    yg_send,
    yg_recv,
    dg_send,
    dg_recv,
):
    me_dp = lax.axis_index("dp")
    me_gx = lax.axis_index("gx")
    gx_count = z_count * Y_RING
    me_z = me_gx // Y_RING
    me_y = me_gx % Y_RING
    left = (me_dp, (me_gx + gx_count - 1) % gx_count)
    right = (me_dp, (me_gx + 1) % gx_count)

    def dp_peer(k):
        return ((me_dp + k) % dp_count, me_gx)

    def y_peer(k):
        return (me_dp, me_z * Y_RING + (me_y + k) % Y_RING)

    def z_peer(k):
        return (me_dp, ((me_z + k) % z_count) * Y_RING + me_y)

    loads = []
    for at, (src, dst) in enumerate(
        (
            (emb_hbm, emb),
            (labels_hbm, labels),
            (feat_hbm.at[0], feat.at[0]),
            (feat_hbm.at[1], feat.at[1]),
            (cot_hbm.at[0], cot.at[0]),
            (cot_hbm.at[1], cot.at[1]),
            (one_hbm, one),
            (two_hbm, two),
        )
    ):
        copy = pltpu.make_async_copy(src, dst, in_sem.at[at])
        copy.start()
        loads.append(copy)

    for field in (base3, hid3):
        for s in range(SAMPLES):
            for plane in range(PLANES + 2):
                low = plane * TRIPLE + CH
                field[s, low : low + CH, 0:SPAN] = jnp.zeros((CH, SPAN), BF16)
                field[s, low : low + CH, PADDED - SPAN : PADDED] = jnp.zeros((CH, SPAN), BF16)
    for at in range(2):
        part[at, :, 0:SPAN] = jnp.zeros((TRIPLE, SPAN), F32)
        part[at, :, PADDED - SPAN : PADDED] = jnp.zeros((TRIPLE, SPAN), F32)

    barrier = pltpu.get_barrier_semaphore()
    peers = [left, right]
    peers += [dp_peer(k) for k in range(1, dp_count)]
    peers += [y_peer(k) for k in range(1, Y_RING)]
    peers += [z_peer(k) for k in range(1, z_count)]
    for peer in peers:
        pl.semaphore_signal(barrier, inc=1, device_id=peer, device_id_type=MESH)

    eye = (
        lax.broadcasted_iota(jnp.int32, (CH, CH), 0) == lax.broadcasted_iota(jnp.int32, (CH, CH), 1)
    ).astype(BF16)
    loads[0].wait()
    loads[1].wait()
    table = emb[...]
    high = table.astype(BF16)
    rest = table - high.astype(F32)
    middle = rest.astype(BF16)
    low = (rest - middle.astype(F32)).astype(BF16)
    pieces = jnp.concatenate(
        [high.astype(F32), middle.astype(F32), low.astype(F32), jnp.zeros((8, CH), F32)], axis=0
    ).astype(BF16)
    turned = lax.dot_general(eye, pieces, NT, preferred_element_type=F32).astype(BF16)

    def widen(source, s):
        def step(c, carry):
            block = source[s, pl.ds(c * 8, 8)].reshape(8 * PLANES * DEPTH, SPAN)
            wide[s, rows(c * 8 * PLANES * DEPTH, 8 * PLANES * DEPTH), :] = block.astype(F32)
            return carry

        lax.fori_loop(0, CH // 8, step, 0)

    def put(field, s, plane, z, value, order):
        before, after = shifted(value)
        first, last = (after, before) if order > 0 else (before, after)
        low = plane * TRIPLE
        lanes = slice((z + 1) * SPAN, (z + 2) * SPAN)
        field[s, rows(low, CH), lanes] = first.astype(BF16)
        field[s, rows(low + CH, CH), lanes] = value.astype(BF16)
        field[s, rows(low + 2 * CH, CH), lanes] = last.astype(BF16)

    def base_plane(s, x):
        kind = lax.broadcasted_iota(jnp.int32, (32, SPAN), 0) % 8
        for z in range(DEPTH):
            row = labels[s, x, z : z + 1, :]
            hot = (jnp.broadcast_to(row, (32, SPAN)) == kind).astype(F32).astype(BF16)
            looked = jnp.dot(turned, hot, preferred_element_type=F32)
            own = wide[s, pl.ds(x * DEPTH + z, CH, stride=PLANES * DEPTH), :]
            put(base3, s, x + 1, z, own + looked, 1)

    def cot_plane(s, x):
        for z in range(DEPTH):
            own = wide[s, pl.ds(x * DEPTH + z, CH, stride=PLANES * DEPTH), :]
            put(cot3, s, x + 1, z, own, -1)

    def halo(field, which, s):
        inner = slice(SPAN, SPAN + CELLS)
        copies = []
        for side, (at, to, device) in enumerate(
            ((1, PLANES + 1, left), (PLANES, 0, right))
        ):
            copies.append(
                pltpu.make_async_remote_copy(
                    src_ref=field.at[s, at * TRIPLE + CH : at * TRIPLE + 2 * CH, inner],
                    dst_ref=field.at[s, to * TRIPLE + CH : to * TRIPLE + 2 * CH, inner],
                    send_sem=halo_send.at[which, s, side],
                    recv_sem=halo_recv.at[which, s, side],
                    device_id=device,
                    device_id_type=MESH,
                )
            )
        return copies

    def halo_shifts(field, s, order):
        for plane in (0, PLANES + 1):
            low = plane * TRIPLE
            own = field[s, low + CH : low + 2 * CH, SPAN : SPAN + CELLS].astype(F32)
            for z in range(DEPTH):
                lanes = slice((z + 1) * SPAN, (z + 2) * SPAN)
                before, after = shifted(own[:, z * SPAN : (z + 1) * SPAN])
                first, last = (after, before) if order > 0 else (before, after)
                field[s, low : low + CH, lanes] = first.astype(BF16)
                field[s, low + 2 * CH : low + TRIPLE, lanes] = last.astype(BF16)

    halos = [[halo(field, which, s) for s in range(SAMPLES)] for which, field in enumerate((base3, cot3, hid3))]

    for s in range(SAMPLES):
        loads[2 + s].wait()
        widen(feat, s)
        for x in range(PLANES):
            base_plane(s, x)
        if s == 0:
            pl.semaphore_wait(barrier, len(peers))
        for copy in halos[0][s]:
            copy.start()
    for s in range(SAMPLES):
        loads[4 + s].wait()
        widen(cot, s)
        for x in range(PLANES):
            cot_plane(s, x)
        for copy in halos[1][s]:
            copy.start()

    loads[6].wait()
    loads[7].wait()
    for b in range(3):
        for source, target in ((one, w_one), (two, w_two)):
            stacked = jnp.concatenate(
                [source[(a * 3 + b) * 3 + e] for a in range(3) for e in range(3)], axis=0
            )
            target[b * CH : (b + 1) * CH, :] = lax.dot_general(
                eye, stacked, NT, preferred_element_type=F32
            ).astype(BF16)
        flat = jnp.concatenate(
            [
                lax.dot_general(
                    eye, two[((2 - a) * 3 + b) * 3 + e], NT, preferred_element_type=F32
                ).astype(BF16)
                for a in range(3)
                for e in range(3)
            ],
            axis=0,
        )
        w_back[b * CH : (b + 1) * CH, :] = lax.dot_general(
            eye, flat, NT, preferred_element_type=F32
        ).astype(BF16)

    def products(field, weights, s, x, at):
        part[at, :, SPAN : SPAN + CELLS] = jnp.dot(
            weights[...],
            field[s, x * TRIPLE : (x + 3) * TRIPLE, SPAN : SPAN + CELLS],
            preferred_element_type=F32,
        )

    def summed(z, order, at):
        total = part[at, CH : 2 * CH, (z + 1) * SPAN : (z + 2) * SPAN]
        total = total + part[at, 0:CH, (z + 1 - order) * SPAN : (z + 2 - order) * SPAN]
        return total + part[at, 2 * CH :, (z + 1 + order) * SPAN : (z + 2 + order) * SPAN]

    def first_layer(s, x, at):
        products(base3, w_one, s, x, at)
        for z in range(DEPTH):
            pre = summed(z, 1, at)
            q = jax.nn.sigmoid(pre)
            factor[s, x, :, z * SPAN : (z + 1) * SPAN] = q * (1.0 + pre * (1.0 - q))
            put(hid3, s, x + 1, z, pre * q, 1)

    def backward(s, x, at):
        products(cot3, w_back, s, x, at)
        for z in range(DEPTH):
            d_pre = summed(z, -1, at) * factor[s, x, :, z * SPAN : (z + 1) * SPAN]
            before, after = shifted(d_pre)
            lanes = slice(z * SPAN, (z + 1) * SPAN)
            low = x * TRIPLE
            dpre3[s, low : low + CH, lanes] = before.astype(BF16)
            dpre3[s, low + CH : low + 2 * CH, lanes] = d_pre.astype(BF16)
            dpre3[s, low + 2 * CH : low + TRIPLE, lanes] = after.astype(BF16)

    def second_layer(s, x, at):
        products(hid3, w_two, s, x, at)
        low = (x + 1) * TRIPLE + CH
        for z in range(DEPTH):
            own = base3[s, low : low + CH, (z + 1) * SPAN : (z + 2) * SPAN]
            wide[s, pl.ds(x * DEPTH + z, CH, stride=PLANES * DEPTH), :] = summed(z, 1, at) + own.astype(F32)

    def planes_of(work, places):
        for i, (s, x) in enumerate(places):
            work(s, x, i % 2)

    inner = [(s, x) for s in range(SAMPLES) for x in range(1, PLANES - 1)]
    edges = [(s, x) for s in range(SAMPLES) for x in (0, PLANES - 1)]

    planes_of(first_layer, inner)
    for s in range(SAMPLES):
        for copy in halos[0][s]:
            copy.wait_recv()
    for s in range(SAMPLES):
        halo_shifts(base3, s, 1)
    planes_of(first_layer, edges)
    for s in range(SAMPLES):
        for copy in halos[2][s]:
            copy.start()
    planes_of(backward, inner)
    for s in range(SAMPLES):
        for copy in halos[1][s]:
            copy.wait_recv()
    for s in range(SAMPLES):
        halo_shifts(cot3, s, -1)
    planes_of(backward, edges)

    def gradient(g, field, partner, partner_plane, partner_lane):
        acc[...] = jnp.zeros_like(acc)

        def step(s, carry):
            taps = jnp.concatenate(
                [
                    jnp.concatenate(
                        [
                            field[
                                s,
                                (x + a) * TRIPLE + CH : (x + a) * TRIPLE + 2 * CH,
                                b * SPAN : b * SPAN + CELLS,
                            ]
                            for x in range(PLANES)
                        ],
                        axis=1,
                    )
                    for a in range(3)
                    for b in range(3)
                ],
                axis=0,
            )
            other = jnp.concatenate(
                [
                    partner[
                        s,
                        (x + partner_plane) * TRIPLE : (x + partner_plane + 1) * TRIPLE,
                        partner_lane : partner_lane + CELLS,
                    ]
                    for x in range(PLANES)
                ],
                axis=1,
            )
            acc[...] += lax.dot_general(taps, other, NT, preferred_element_type=F32)
            return carry

        lax.fori_loop(0, SAMPLES, step, 0)
        half = 9 * CH // 2
        packed[g, 0 : 9 * CH, :] = acc[:, 0:SPAN].astype(BF16)
        packed[g, 9 * CH : 9 * CH + half, :] = jnp.concatenate(
            [acc[0:half, SPAN:TRIPLE], acc[half : 2 * half, SPAN:TRIPLE]], axis=1
        ).astype(BF16)
        packed[g, 9 * CH + half :, :] = jnp.zeros((PACKED - 9 * CH - half, SPAN), BF16)

    dp_rows = PACKED // dp_count
    y_rows = dp_rows // Y_RING

    def sum_dp(g):
        return [
            pltpu.make_async_remote_copy(
                src_ref=packed.at[g, rows(((me_dp + k) % dp_count) * dp_rows, dp_rows)],
                dst_ref=got_dp.at[g, k - 1],
                send_sem=dp_send.at[g, k - 1],
                recv_sem=dp_recv.at[g, k - 1],
                device_id=dp_peer(k),
                device_id_type=MESH,
            )
            for k in range(1, dp_count)
        ]

    def sum_y(g):
        return [
            pltpu.make_async_remote_copy(
                src_ref=mine_y.at[g, rows(((me_y + k) % Y_RING) * y_rows, y_rows)],
                dst_ref=got_y.at[g, k - 1],
                send_sem=y_send.at[g, k - 1],
                recv_sem=y_recv.at[g, k - 1],
                device_id=y_peer(k),
                device_id_type=MESH,
            )
            for k in range(1, Y_RING)
        ]

    def spread_z(g):
        return [
            pltpu.make_async_remote_copy(
                src_ref=all_z.at[g, me_z],
                dst_ref=all_z.at[g, me_z],
                send_sem=z_send.at[g, k - 1],
                recv_sem=z_recv.at[g, k - 1],
                device_id=z_peer(k),
                device_id_type=MESH,
            )
            for k in range(1, z_count)
        ]

    def my_y_rows():
        return rows(me_dp * dp_rows + me_y * y_rows, y_rows)

    def my_dp_rows():
        return rows(me_dp * dp_rows, dp_rows)

    def gather_y(g):
        return [
            pltpu.make_async_remote_copy(
                src_ref=full.at[g, my_y_rows()],
                dst_ref=full.at[g, my_y_rows()],
                send_sem=yg_send.at[g, k - 1],
                recv_sem=yg_recv.at[g, k - 1],
                device_id=y_peer(k),
                device_id_type=MESH,
            )
            for k in range(1, Y_RING)
        ]

    def gather_dp(g):
        return [
            pltpu.make_async_remote_copy(
                src_ref=full.at[g, my_dp_rows()],
                dst_ref=full.at[g, my_dp_rows()],
                send_sem=dg_send.at[g, k - 1],
                recv_sem=dg_recv.at[g, k - 1],
                device_id=dp_peer(k),
                device_id_type=MESH,
            )
            for k in range(1, dp_count)
        ]

    sent = []

    def start(copies):
        for copy in copies:
            copy.start()
        sent.extend(copies)
        return copies

    def arrived(copies):
        for copy in copies:
            copy.wait_recv()

    def stage_one(g, dp_copies):
        arrived(dp_copies)
        total = packed[g, my_dp_rows(), :].astype(F32)
        for k in range(dp_count - 1):
            total = total + got_dp[g, k].astype(F32)
        mine_y[g] = total.astype(BF16)
        return start(sum_y(g))

    def stage_two(g, y_copies):
        arrived(y_copies)
        total = mine_y[g, rows(me_y * y_rows, y_rows), :].astype(F32)
        for k in range(Y_RING - 1):
            total = total + got_y[g, k].astype(F32)
        all_z[g, me_z] = total.astype(BF16)
        return start(spread_z(g))

    def stage_three(g, z_copies):
        arrived(z_copies)
        total = all_z[g, 0].astype(F32)
        for k in range(1, z_count):
            total = total + all_z[g, k].astype(F32)
        full[g, my_y_rows(), :] = (total * scale).astype(BF16)
        return start(gather_y(g))

    def stage_four(g, yg_copies):
        arrived(yg_copies)
        return start(gather_dp(g))

    gradient(0, base3, dpre3, 0, 0)
    wait_zero = start(sum_dp(0))
    for s in range(SAMPLES):
        for copy in halos[2][s]:
            copy.wait_recv()
        halo_shifts(hid3, s, 1)
    gradient(1, hid3, cot3, 1, SPAN)
    wait_one = start(sum_dp(1))
    wait_zero = stage_one(0, wait_zero)

    def give_back(s):
        def step(c, carry):
            block = wide[s, rows(c * 8 * PLANES * DEPTH, 8 * PLANES * DEPTH), :]
            held[s, pl.ds(c * 8, 8)] = block.reshape(8, PLANES * DEPTH, SPAN).astype(BF16)
            return carry

        lax.fori_loop(0, CH // 8, step, 0)

    planes_of(second_layer, [(0, x) for x in range(PLANES)])
    wait_one = stage_one(1, wait_one)
    wait_zero = stage_two(0, wait_zero)
    give_back(0)
    planes_of(second_layer, [(1, x) for x in range(PLANES)])
    wait_one = stage_two(1, wait_one)
    wait_zero = stage_three(0, wait_zero)
    give_back(1)
    wait_one = stage_three(1, wait_one)
    wait_zero = stage_four(0, wait_zero)
    wait_one = stage_four(1, wait_one)
    arrived(wait_zero)
    arrived(wait_one)

    for field in halos:
        for side in field:
            for copy in side:
                copy.wait_send()
    for copy in sent:
        copy.wait_send()


def finish(held, sums, out_hbm, grad_one, grad_two, spread, sems):
    copies = [pltpu.make_async_copy(held, out_hbm, sems.at[0])]
    copies[0].start()
    half = 9 * CH // 2
    for g, target in enumerate((grad_one, grad_two)):
        for tap in range(9):
            block = sums[g, tap * CH : (tap + 1) * CH, :].astype(F32)
            spread[g, tap * 3] = block[:, 0:CH]
            spread[g, tap * 3 + 1] = block[:, CH:]
        for piece in range(18):
            low = piece * 32
            lane = 0
            if low >= half:
                low, lane = low - half, CH
            block = sums[g, 9 * CH + low : 9 * CH + low + 32, lane : lane + CH].astype(F32)
            spread[g, (piece // 2) * 3 + 2, (piece % 2) * 32 : (piece % 2) * 32 + 32, :] = block
        copies.append(pltpu.make_async_copy(spread.at[g], target, sems.at[1 + g]))
        copies[-1].start()
    for copy in copies:
        copy.wait()


def on_device(dp_count, z_count, features, labels, embedding, weight_one, weight_two, cotangent):
    count = SAMPLES * dp_count * PLANES * z_count * Y_RING * CELLS
    dp_rows = PACKED // dp_count
    y_rows = dp_rows // Y_RING
    flat = (SAMPLES, CH, PLANES * DEPTH, SPAN)
    dma = pltpu.SemaphoreType.DMA
    field = pltpu.VMEM((SAMPLES, (PLANES + 2) * TRIPLE, PADDED), BF16)
    held, sums = pl.pallas_call(
        functools.partial(body, dp_count, z_count, 1.0 / math.sqrt(count)),
        out_shape=(pltpu.VMEM(flat, BF16), pltpu.VMEM((2, PACKED, SPAN), BF16)),
        in_specs=[pl.BlockSpec(memory_space=pltpu.HBM)] * 6,
        out_specs=(pl.BlockSpec(memory_space=pltpu.VMEM),) * 2,
        scratch_shapes=[
            pltpu.VMEM(flat, BF16),
            pltpu.VMEM(flat, BF16),
            pltpu.VMEM((SAMPLES, PLANES, DEPTH, SPAN), jnp.int32),
            pltpu.VMEM((8, CH), F32),
            pltpu.VMEM((27, CH, CH), BF16),
            pltpu.VMEM((27, CH, CH), BF16),
            pltpu.VMEM((SAMPLES, CH * PLANES * DEPTH, SPAN), F32),
            field,
            field,
            field,
            pltpu.VMEM((SAMPLES, PLANES * TRIPLE, CELLS), BF16),
            pltpu.VMEM((SAMPLES, PLANES, CH, CELLS), F32),
            pltpu.VMEM((2, TRIPLE, PADDED), F32),
            pltpu.VMEM((TRIPLE, 3 * TRIPLE), BF16),
            pltpu.VMEM((TRIPLE, 3 * TRIPLE), BF16),
            pltpu.VMEM((TRIPLE, 3 * TRIPLE), BF16),
            pltpu.VMEM((9 * CH, TRIPLE), F32),
            pltpu.VMEM((2, PACKED, SPAN), BF16),
            pltpu.VMEM((2, dp_count - 1, dp_rows, SPAN), BF16),
            pltpu.VMEM((2, dp_rows, SPAN), BF16),
            pltpu.VMEM((2, Y_RING - 1, y_rows, SPAN), BF16),
            pltpu.VMEM((2, z_count, y_rows, SPAN), BF16),
            dma((8,)),
            dma((3, SAMPLES, 2)),
            dma((3, SAMPLES, 2)),
            dma((2, dp_count - 1)),
            dma((2, dp_count - 1)),
            dma((2, Y_RING - 1)),
            dma((2, Y_RING - 1)),
            dma((2, max(z_count - 1, 1))),
            dma((2, max(z_count - 1, 1))),
            dma((2, Y_RING - 1)),
            dma((2, Y_RING - 1)),
            dma((2, dp_count - 1)),
            dma((2, dp_count - 1)),
        ],
        compiler_params=pltpu.CompilerParams(
            collective_id=0, has_side_effects=True, vmem_limit_bytes=56 * 1024 * 1024
        ),
        name="surrogate",
    )(
        features.reshape(flat),
        labels,
        embedding,
        weight_one.reshape(27, CH, CH),
        weight_two.reshape(27, CH, CH),
        cotangent.reshape(flat),
    )
    output, grad_one, grad_two = pl.pallas_call(
        finish,
        out_shape=(
            jax.ShapeDtypeStruct(flat, BF16),
            jax.ShapeDtypeStruct((27, CH, CH), F32),
            jax.ShapeDtypeStruct((27, CH, CH), F32),
        ),
        in_specs=[pl.BlockSpec(memory_space=pltpu.VMEM)] * 2,
        out_specs=(pl.BlockSpec(memory_space=pltpu.HBM),) * 3,
        scratch_shapes=[pltpu.VMEM((2, 27, CH, CH), F32), dma((3,))],
        compiler_params=pltpu.CompilerParams(vmem_limit_bytes=16 * 1024 * 1024),
        name="finish",
    )(held, sums)
    taps = (3, 3, 3, CH, CH)
    return output.reshape(features.shape), grad_one.reshape(taps), grad_two.reshape(taps)


def solution(mesh):
    dp_count = mesh.shape["dp"]
    z_count = mesh.shape["gx"] // Y_RING
    placed = (
        P("dp", None, "gx", None, None),
        P("dp", "gx", None, None),
        P(),
        P(),
        P(),
        P("dp", None, "gx", None, None),
    )
    return jax.shard_map(
        functools.partial(on_device, dp_count, z_count),
        mesh=mesh,
        in_specs=placed,
        out_specs=(P("dp", None, "gx", None, None), P(), P()),
        check_vma=False,
    )
```

```python
import functools
import math

import jax
import jax.numpy as jnp
from jax import lax
from jax.experimental import pallas as pl
from jax.experimental.pallas import tpu as pltpu
from jax.sharding import PartitionSpec as P

MESH = pl.DeviceIdType.MESH
F32 = jnp.float32
BF16 = jnp.bfloat16

CH = 64
PLANES = 4
DEPTH = 8
SPAN = 128
CELLS = DEPTH * SPAN
PADDED = CELLS + 2 * SPAN
TRIPLE = 3 * CH
SAMPLES = 2
PACKED = 1024
Y_RING = 4
NT = (((1,), (1,)), ((), ()))


def rows(start, size, unit=16):
    return pl.ds(pl.multiple_of(start, unit), size)


def shifted(value):
    lane = lax.broadcasted_iota(jnp.int32, value.shape, 1)
    after = jnp.where(lane == 0, 0.0, pltpu.roll(value, 1, 1))
    before = jnp.where(lane == SPAN - 1, 0.0, pltpu.roll(value, SPAN - 1, 1))
    return before, after


def body(
    dp_count,
    z_count,
    scale,
    feat_hbm,
    labels_hbm,
    emb_hbm,
    one_hbm,
    two_hbm,
    cot_hbm,
    held,
    full,
    feat,
    cot,
    labels,
    emb,
    one,
    two,
    wide,
    base3,
    cot3,
    hid3,
    dpre3,
    factor,
    part,
    w_one,
    w_two,
    w_back,
    acc,
    packed,
    got_core,
    mine,
    got_xy,
    all_z,
    in_sem,
    halo_send,
    halo_recv,
    *links,
):
    sum_core, sum_xy, sum_z, back_xy, back_core = zip(links[0::2], links[1::2])
    me_dp = lax.axis_index("dp")
    me_gx = lax.axis_index("gx")
    gx_count = z_count * Y_RING
    me_z = me_gx // Y_RING
    me_y = me_gx % Y_RING
    left = (me_dp, (me_gx + gx_count - 1) % gx_count)
    right = (me_dp, (me_gx + 1) % gx_count)

    x_count = dp_count // 2
    me_x = me_dp // 2
    me_core = me_dp % 2
    xy_count = x_count * Y_RING
    me_xy = me_x * Y_RING + me_y
    sibling = (me_x * 2 + 1 - me_core, me_gx)

    def xy_peer(k):
        to = (me_xy + k) % xy_count
        return ((to // Y_RING) * 2 + me_core, me_z * Y_RING + to % Y_RING)

    def z_peer(k):
        return (me_dp, ((me_z + k) % z_count) * Y_RING + me_y)

    loads = []
    for at, (src, dst) in enumerate(
        (
            (emb_hbm, emb),
            (labels_hbm, labels),
            (feat_hbm.at[0], feat.at[0]),
            (feat_hbm.at[1], feat.at[1]),
            (cot_hbm.at[0], cot.at[0]),
            (cot_hbm.at[1], cot.at[1]),
            (one_hbm, one),
            (two_hbm, two),
        )
    ):
        copy = pltpu.make_async_copy(src, dst, in_sem.at[at])
        copy.start()
        loads.append(copy)

    for field in (base3, cot3):
        for s in range(SAMPLES):
            for plane in range(PLANES + 2):
                low = plane * TRIPLE + CH
                field[s, low : low + CH, 0:SPAN] = jnp.zeros((CH, SPAN), BF16)
                field[s, low : low + CH, PADDED - SPAN : PADDED] = jnp.zeros((CH, SPAN), BF16)
    for at in range(2):
        part[at, :, 0:SPAN] = jnp.zeros((TRIPLE, SPAN), F32)
        part[at, :, PADDED - SPAN : PADDED] = jnp.zeros((TRIPLE, SPAN), F32)

    barrier = pltpu.get_barrier_semaphore()
    peers = [left, right, sibling]
    peers += [xy_peer(k) for k in range(1, xy_count)]
    peers += [z_peer(k) for k in range(1, z_count)]
    for peer in peers:
        pl.semaphore_signal(barrier, inc=1, device_id=peer, device_id_type=MESH)

    eye = (
        lax.broadcasted_iota(jnp.int32, (CH, CH), 0) == lax.broadcasted_iota(jnp.int32, (CH, CH), 1)
    ).astype(BF16)
    loads[0].wait()
    loads[1].wait()
    table = emb[...]
    high = table.astype(BF16)
    rest = table - high.astype(F32)
    middle = rest.astype(BF16)
    low = (rest - middle.astype(F32)).astype(BF16)
    pieces = jnp.concatenate(
        [high.astype(F32), middle.astype(F32), low.astype(F32), jnp.zeros((8, CH), F32)], axis=0
    ).astype(BF16)
    turned = lax.dot_general(eye, pieces, NT, preferred_element_type=F32).astype(BF16)

    def widen(source, s):
        def step(c, carry):
            block = source[s, pl.ds(c * 8, 8)].reshape(8 * PLANES * DEPTH, SPAN)
            wide[s, rows(c * 8 * PLANES * DEPTH, 8 * PLANES * DEPTH), :] = block.astype(F32)
            return carry

        lax.fori_loop(0, CH // 8, step, 0)

    def put(field, s, plane, z, value, order):
        before, after = shifted(value)
        first, last = (after, before) if order > 0 else (before, after)
        low = plane * TRIPLE
        lanes = slice((z + 1) * SPAN, (z + 2) * SPAN)
        field[s, rows(low, CH), lanes] = first.astype(BF16)
        field[s, rows(low + CH, CH), lanes] = value.astype(BF16)
        field[s, rows(low + 2 * CH, CH), lanes] = last.astype(BF16)

    def base_plane(s, x):
        kind = lax.broadcasted_iota(jnp.int32, (32, SPAN), 0) % 8
        for z in range(DEPTH):
            row = labels[s, x, z : z + 1, :]
            hot = (jnp.broadcast_to(row, (32, SPAN)) == kind).astype(F32).astype(BF16)
            looked = jnp.dot(turned, hot, preferred_element_type=F32)
            own = wide[s, pl.ds(x * DEPTH + z, CH, stride=PLANES * DEPTH), :]
            put(base3, s, x + 1, z, own + looked, 1)

    def cot_plane(s, x):
        for z in range(DEPTH):
            own = wide[s, pl.ds(x * DEPTH + z, CH, stride=PLANES * DEPTH), :]
            put(cot3, s, x + 1, z, own, -1)

    def halo(field, which, s):
        inner = slice(SPAN, SPAN + CELLS)
        copies = []
        for side, (at, to, device) in enumerate(
            ((1, PLANES + 1, left), (PLANES, 0, right))
        ):
            copies.append(
                pltpu.make_async_remote_copy(
                    src_ref=field.at[s, at * TRIPLE + CH : at * TRIPLE + 2 * CH, inner],
                    dst_ref=field.at[s, to * TRIPLE + CH : to * TRIPLE + 2 * CH, inner],
                    send_sem=halo_send.at[which, s, side],
                    recv_sem=halo_recv.at[which, s, side],
                    device_id=device,
                    device_id_type=MESH,
                )
            )
        return copies

    def halo_shifts(field, s, order):
        for plane in (0, PLANES + 1):
            low = plane * TRIPLE
            own = field[s, low + CH : low + 2 * CH, SPAN : SPAN + CELLS].astype(F32)
            for z in range(DEPTH):
                lanes = slice((z + 1) * SPAN, (z + 2) * SPAN)
                before, after = shifted(own[:, z * SPAN : (z + 1) * SPAN])
                first, last = (after, before) if order > 0 else (before, after)
                field[s, low : low + CH, lanes] = first.astype(BF16)
                field[s, low + 2 * CH : low + TRIPLE, lanes] = last.astype(BF16)

    halos = [[halo(field, which, s) for s in range(SAMPLES)] for which, field in enumerate((base3, cot3, hid3))]

    for s in range(SAMPLES):
        loads[2 + s].wait()
        widen(feat, s)
        for x in range(PLANES):
            base_plane(s, x)
        if s == 0:
            pl.semaphore_wait(barrier, len(peers))
        for copy in halos[0][s]:
            copy.start()
    for s in range(SAMPLES):
        loads[4 + s].wait()
        widen(cot, s)
        for x in range(PLANES):
            cot_plane(s, x)
        for copy in halos[1][s]:
            copy.start()

    loads[6].wait()
    loads[7].wait()
    for b in range(3):
        for source, target in ((one, w_one), (two, w_two)):
            stacked = jnp.concatenate(
                [source[(a * 3 + b) * 3 + e] for a in range(3) for e in range(3)], axis=0
            )
            target[b * CH : (b + 1) * CH, :] = lax.dot_general(
                eye, stacked, NT, preferred_element_type=F32
            ).astype(BF16)
        flat = jnp.concatenate(
            [
                lax.dot_general(
                    eye, two[((2 - a) * 3 + b) * 3 + e], NT, preferred_element_type=F32
                ).astype(BF16)
                for a in range(3)
                for e in range(3)
            ],
            axis=0,
        )
        w_back[b * CH : (b + 1) * CH, :] = lax.dot_general(
            eye, flat, NT, preferred_element_type=F32
        ).astype(BF16)

    def products(field, weights, s, x, at):
        part[at, :, SPAN : SPAN + CELLS] = jnp.dot(
            weights[...],
            field[s, x * TRIPLE : (x + 3) * TRIPLE, SPAN : SPAN + CELLS],
            preferred_element_type=F32,
        )

    def summed(z, order, at):
        total = part[at, CH : 2 * CH, (z + 1) * SPAN : (z + 2) * SPAN]
        total = total + part[at, 0:CH, (z + 1 - order) * SPAN : (z + 2 - order) * SPAN]
        return total + part[at, 2 * CH :, (z + 1 + order) * SPAN : (z + 2 + order) * SPAN]

    def first_layer(s, x, at):
        products(base3, w_one, s, x, at)
        for z in range(DEPTH):
            pre = summed(z, 1, at)
            q = jax.nn.sigmoid(pre)
            factor[s, x, :, z * SPAN : (z + 1) * SPAN] = q * (1.0 + pre * (1.0 - q))
            put(hid3, s, x + 1, z, pre * q, 1)

    def backward(s, x, at):
        products(cot3, w_back, s, x, at)
        for z in range(DEPTH):
            d_pre = summed(z, -1, at) * factor[s, x, :, z * SPAN : (z + 1) * SPAN]
            before, after = shifted(d_pre)
            lanes = slice(z * SPAN, (z + 1) * SPAN)
            low = x * TRIPLE
            dpre3[s, low : low + CH, lanes] = before.astype(BF16)
            dpre3[s, low + CH : low + 2 * CH, lanes] = d_pre.astype(BF16)
            dpre3[s, low + 2 * CH : low + TRIPLE, lanes] = after.astype(BF16)

    def second_layer(s, x, at):
        products(hid3, w_two, s, x, at)
        low = (x + 1) * TRIPLE + CH
        for z in range(DEPTH):
            own = base3[s, low : low + CH, (z + 1) * SPAN : (z + 2) * SPAN]
            wide[s, pl.ds(x * DEPTH + z, CH, stride=PLANES * DEPTH), :] = summed(z, 1, at) + own.astype(F32)

    def planes_of(work, places):
        for i, (s, x) in enumerate(places):
            work(s, x, i % 2)

    inner = [(s, x) for s in range(SAMPLES) for x in range(1, PLANES - 1)]
    edges = [(s, x) for s in range(SAMPLES) for x in (0, PLANES - 1)]

    def gradient(total, taps_of, others_of, places):
        taps = jnp.concatenate(
            [
                jnp.concatenate([taps_of(s, x, a, b) for s, x in places], axis=1)
                for a in range(3)
                for b in range(3)
            ],
            axis=0,
        )
        others = jnp.concatenate([others_of(s, x) for s, x in places], axis=1)
        return total + lax.dot_general(taps, others, NT, preferred_element_type=F32)

    def base_taps(s, x, a, b):
        low = (x + a) * TRIPLE + CH
        return base3[s, low : low + CH, b * SPAN : b * SPAN + CELLS]

    def d_pre_of(s, x):
        return dpre3[s, x * TRIPLE : (x + 1) * TRIPLE, :]

    def cot_taps(s, x, a, b):
        low = (x + 2 - a) * TRIPLE + CH
        return cot3[s, low : low + CH, (2 - b) * SPAN : (2 - b) * SPAN + CELLS]

    def hidden_of(s, x):
        return hid3[s, (x + 1) * TRIPLE : (x + 2) * TRIPLE, SPAN : SPAN + CELLS]

    def pack(g, total):
        packed[g, 0 : 9 * CH, :] = total[:, 0:SPAN].astype(BF16)
        last = total[:, SPAN:TRIPLE]
        for pair in range(5):
            one_tap = last[2 * pair * CH : (2 * pair + 1) * CH]
            next_tap = last[(2 * pair + 1) * CH : (2 * pair + 2) * CH] if pair < 4 else jnp.zeros_like(one_tap)
            low = (9 + pair) * CH
            packed[g, low : low + CH, :] = jnp.concatenate([one_tap, next_tap], axis=1).astype(BF16)
        packed[g, 14 * CH :, :] = jnp.zeros((PACKED - 14 * CH, SPAN), BF16)

    half = PACKED // 2
    chunk = half // xy_count

    def remote(src, dst, sems, at, peer):
        return pltpu.make_async_remote_copy(
            src_ref=src,
            dst_ref=dst,
            send_sem=sems[0].at[at],
            recv_sem=sems[1].at[at],
            device_id=peer,
            device_id_type=MESH,
        )

    sent = []

    def start(copies):
        for copy in copies:
            copy.start()
        sent.extend(copies)
        return copies

    def arrived(copies):
        for copy in copies:
            copy.wait_recv()

    def my_half():
        return rows(me_core * half, half)

    def my_chunk():
        return rows(me_core * half + me_xy * chunk, chunk)

    def to_sibling(g):
        src = packed.at[g, rows((1 - me_core) * half, half)]
        return start([remote(src, got_core.at[g], sum_core, g, sibling)])

    def spread_xy(g, copies):
        arrived(copies)
        total = packed[g, my_half(), :].astype(F32) + got_core[g].astype(F32)
        mine[g] = total.astype(BF16)
        copies = []
        for k in range(1, xy_count):
            src = mine.at[g, rows(((me_xy + k) % xy_count) * chunk, chunk)]
            copies.append(remote(src, got_xy.at[g, k - 1], sum_xy, (g, k - 1), xy_peer(k)))
        return start(copies)

    def spread_z(waits):
        for g, copies in enumerate(waits):
            arrived(copies)
            total = mine[g, rows(me_xy * chunk, chunk), :].astype(F32)
            for k in range(xy_count - 1):
                total = total + got_xy[g, k].astype(F32)
            all_z[me_z, g] = total.astype(BF16)
        own = all_z.at[me_z]
        return start([remote(own, own, sum_z, k - 1, z_peer(k)) for k in range(1, z_count)])

    def gather_xy(copies):
        arrived(copies)
        total = all_z[0].astype(F32)
        for k in range(1, z_count):
            total = total + all_z[k].astype(F32)
        full[:, my_chunk(), :] = (total * scale).astype(BF16)
        own = full.at[:, my_chunk()]
        return start([remote(own, own, back_xy, k - 1, xy_peer(k)) for k in range(1, xy_count)])

    def gather_core(copies):
        arrived(copies)
        own = full.at[:, my_half()]
        return start([remote(own, own, back_core, 0, sibling)])

    def give_back(s):
        def step(c, carry):
            block = wide[s, rows(c * 8 * PLANES * DEPTH, 8 * PLANES * DEPTH), :]
            held[s, pl.ds(c * 8, 8)] = block.reshape(8, PLANES * DEPTH, SPAN).astype(BF16)
            return carry

        lax.fori_loop(0, CH // 8, step, 0)

    planes_of(first_layer, inner)
    planes_of(backward, inner)
    acc[1] = gradient(0.0, cot_taps, hidden_of, inner)
    for s in range(SAMPLES):
        for copy in halos[0][s]:
            copy.wait_recv()
    for s in range(SAMPLES):
        halo_shifts(base3, s, 1)
    planes_of(first_layer, edges)
    for s in range(SAMPLES):
        for copy in halos[2][s]:
            copy.start()
    acc[0] = gradient(0.0, base_taps, d_pre_of, inner)
    for s in range(SAMPLES):
        for copy in halos[1][s]:
            copy.wait_recv()
    for s in range(SAMPLES):
        halo_shifts(cot3, s, -1)
    planes_of(backward, edges)
    pack(0, gradient(acc[0], base_taps, d_pre_of, edges))
    core_zero = to_sibling(0)
    pack(1, gradient(acc[1], cot_taps, hidden_of, edges))
    core_one = to_sibling(1)
    xy_zero = spread_xy(0, core_zero)
    planes_of(second_layer, inner)
    xy_one = spread_xy(1, core_one)
    for s in range(SAMPLES):
        for copy in halos[2][s]:
            copy.wait_recv()
    for s in range(SAMPLES):
        halo_shifts(hid3, s, 1)
    planes_of(second_layer, edges)
    waits = spread_z((xy_zero, xy_one))
    give_back(0)
    give_back(1)
    waits = gather_xy(waits)
    waits = gather_core(waits)
    arrived(waits)

    for field in halos:
        for side in field:
            for copy in side:
                copy.wait_send()
    for copy in sent:
        copy.wait_send()


def finish(held, sums, out_hbm, grad_one, grad_two, spread, sems):
    copies = [pltpu.make_async_copy(held, out_hbm, sems.at[0])]
    copies[0].start()
    eye = (
        lax.broadcasted_iota(jnp.int32, (SPAN, SPAN), 0)
        == lax.broadcasted_iota(jnp.int32, (SPAN, SPAN), 1)
    ).astype(BF16)
    for g, target in enumerate((grad_one, grad_two)):
        for piece in range(14):
            block = sums[g, piece * CH : (piece + 1) * CH, :]
            if g == 0:
                block = block.astype(F32)
                pair = (block[:, 0:CH], block[:, CH:])
            else:
                block = lax.dot_general(eye, block, NT, preferred_element_type=F32)
                pair = (block[0:CH], block[CH:])
            if piece < 9:
                spread[g, piece * 3] = pair[0]
                spread[g, piece * 3 + 1] = pair[1]
            else:
                tap = 2 * (piece - 9)
                spread[g, tap * 3 + 2] = pair[0]
                if tap < 8:
                    spread[g, tap * 3 + 5] = pair[1]
        copies.append(pltpu.make_async_copy(spread.at[g], target, sems.at[1 + g]))
        copies[-1].start()
    for copy in copies:
        copy.wait()


def on_device(dp_count, z_count, features, labels, embedding, weight_one, weight_two, cotangent):
    count = SAMPLES * dp_count * PLANES * z_count * Y_RING * CELLS
    half = PACKED // 2
    xy_count = dp_count // 2 * Y_RING
    chunk = half // xy_count
    flat = (SAMPLES, CH, PLANES * DEPTH, SPAN)
    dma = pltpu.SemaphoreType.DMA
    field = pltpu.VMEM((SAMPLES, (PLANES + 2) * TRIPLE, PADDED), BF16)
    held, sums = pl.pallas_call(
        functools.partial(body, dp_count, z_count, 1.0 / math.sqrt(count)),
        out_shape=(pltpu.VMEM(flat, BF16), pltpu.VMEM((2, PACKED, SPAN), BF16)),
        in_specs=[pl.BlockSpec(memory_space=pltpu.HBM)] * 6,
        out_specs=(pl.BlockSpec(memory_space=pltpu.VMEM),) * 2,
        scratch_shapes=[
            pltpu.VMEM(flat, BF16),
            pltpu.VMEM(flat, BF16),
            pltpu.VMEM((SAMPLES, PLANES, DEPTH, SPAN), jnp.int32),
            pltpu.VMEM((8, CH), F32),
            pltpu.VMEM((27, CH, CH), BF16),
            pltpu.VMEM((27, CH, CH), BF16),
            pltpu.VMEM((SAMPLES, CH * PLANES * DEPTH, SPAN), F32),
            field,
            field,
            field,
            pltpu.VMEM((SAMPLES, PLANES * TRIPLE, CELLS), BF16),
            pltpu.VMEM((SAMPLES, PLANES, CH, CELLS), F32),
            pltpu.VMEM((2, TRIPLE, PADDED), F32),
            pltpu.VMEM((TRIPLE, 3 * TRIPLE), BF16),
            pltpu.VMEM((TRIPLE, 3 * TRIPLE), BF16),
            pltpu.VMEM((TRIPLE, 3 * TRIPLE), BF16),
            pltpu.VMEM((2, 9 * CH, TRIPLE), F32),
            pltpu.VMEM((2, PACKED, SPAN), BF16),
            pltpu.VMEM((2, half, SPAN), BF16),
            pltpu.VMEM((2, half, SPAN), BF16),
            pltpu.VMEM((2, xy_count - 1, chunk, SPAN), BF16),
            pltpu.VMEM((z_count, 2, chunk, SPAN), BF16),
            dma((8,)),
            dma((3, SAMPLES, 2)),
            dma((3, SAMPLES, 2)),
        ]
        + [
            dma(shape)
            for shape in ((2,), (2, xy_count - 1), (max(z_count - 1, 1),), (xy_count - 1,), (1,))
            for _ in range(2)
        ],
        compiler_params=pltpu.CompilerParams(
            collective_id=0, has_side_effects=True, vmem_limit_bytes=56 * 1024 * 1024
        ),
        name="surrogate",
    )(
        features.reshape(flat),
        labels,
        embedding,
        weight_one.reshape(27, CH, CH),
        weight_two.reshape(27, CH, CH),
        cotangent.reshape(flat),
    )
    output, grad_one, grad_two = pl.pallas_call(
        finish,
        out_shape=(
            jax.ShapeDtypeStruct(flat, BF16),
            jax.ShapeDtypeStruct((27, CH, CH), F32),
            jax.ShapeDtypeStruct((27, CH, CH), F32),
        ),
        in_specs=[pl.BlockSpec(memory_space=pltpu.VMEM)] * 2,
        out_specs=(pl.BlockSpec(memory_space=pltpu.HBM),) * 3,
        scratch_shapes=[pltpu.VMEM((2, 27, CH, CH), F32), dma((3,))],
        compiler_params=pltpu.CompilerParams(vmem_limit_bytes=16 * 1024 * 1024),
        name="finish",
    )(held, sums)
    taps = (3, 3, 3, CH, CH)
    return output.reshape(features.shape), grad_one.reshape(taps), grad_two.reshape(taps)


def solution(mesh):
    dp_count = mesh.shape["dp"]
    z_count = mesh.shape["gx"] // Y_RING
    placed = (
        P("dp", None, "gx", None, None),
        P("dp", "gx", None, None),
        P(),
        P(),
        P(),
        P("dp", None, "gx", None, None),
    )
    return jax.shard_map(
        functools.partial(on_device, dp_count, z_count),
        mesh=mesh,
        in_specs=placed,
        out_specs=(P("dp", None, "gx", None, None), P(), P()),
        check_vma=False,
    )
```

```python
import functools
import math

import jax
import jax.numpy as jnp
from jax import lax
from jax.experimental import pallas as pl
from jax.experimental.pallas import tpu as pltpu
from jax.sharding import PartitionSpec as P

MESH = pl.DeviceIdType.MESH
F32 = jnp.float32
BF16 = jnp.bfloat16

CH = 64
PLANES = 4
DEPTH = 8
SPAN = 128
CELLS = DEPTH * SPAN
PADDED = CELLS + 2 * SPAN
TRIPLE = 3 * CH
SAMPLES = 2
PACKED = 1024
Y_RING = 4
NT = (((1,), (1,)), ((), ()))


def rows(start, size, unit=16):
    return pl.ds(pl.multiple_of(start, unit), size)


def shifted(value):
    lane = lax.broadcasted_iota(jnp.int32, value.shape, 1)
    after = jnp.where(lane == 0, 0.0, pltpu.roll(value, 1, 1))
    before = jnp.where(lane == SPAN - 1, 0.0, pltpu.roll(value, SPAN - 1, 1))
    return before, after


def body(
    dp_count,
    z_count,
    scale,
    feat_hbm,
    labels_hbm,
    emb_hbm,
    one_hbm,
    two_hbm,
    cot_hbm,
    held,
    full,
    feat,
    cot,
    labels,
    emb,
    one,
    two,
    wide,
    base3,
    cot3,
    hid3,
    dpre3,
    factor,
    part,
    w_one,
    w_two,
    w_back,
    w_tail,
    acc,
    packed,
    got_core,
    mine,
    got_xy,
    all_z,
    in_sem,
    halo_send,
    halo_recv,
    *links,
):
    sum_core, sum_xy, sum_z, back_xy, back_core = zip(links[0::2], links[1::2])
    me_dp = lax.axis_index("dp")
    me_gx = lax.axis_index("gx")
    gx_count = z_count * Y_RING
    me_z = me_gx // Y_RING
    me_y = me_gx % Y_RING
    left = (me_dp, (me_gx + gx_count - 1) % gx_count)
    right = (me_dp, (me_gx + 1) % gx_count)

    x_count = dp_count // 2
    me_x = me_dp // 2
    me_core = me_dp % 2
    xy_count = x_count * Y_RING
    me_xy = me_x * Y_RING + me_y
    sibling = (me_x * 2 + 1 - me_core, me_gx)

    def hops(offset, count):
        return min(offset, count - offset)

    xy_offsets = sorted(
        ((dx, dy) for dx in range(x_count) for dy in range(Y_RING) if (dx, dy) != (0, 0)),
        key=lambda at: -(hops(at[0], x_count) + hops(at[1], Y_RING)),
    )
    z_offsets = sorted(range(1, z_count), key=lambda at: -hops(at, z_count))

    def xy_place(at):
        return (me_x + at[0]) % x_count, (me_y + at[1]) % Y_RING

    def xy_peer(at):
        x, y = xy_place(at)
        return (x * 2 + me_core, me_z * Y_RING + y)

    def xy_index(at):
        x, y = xy_place(at)
        return x * Y_RING + y

    def z_peer(k):
        return (me_dp, ((me_z + k) % z_count) * Y_RING + me_y)

    loads = []
    for at, (src, dst) in enumerate(
        (
            (emb_hbm, emb),
            (labels_hbm, labels),
            (feat_hbm.at[0], feat.at[0]),
            (feat_hbm.at[1], feat.at[1]),
            (cot_hbm.at[0], cot.at[0]),
            (cot_hbm.at[1], cot.at[1]),
            (one_hbm, one),
            (two_hbm, two),
        )
    ):
        copy = pltpu.make_async_copy(src, dst, in_sem.at[at])
        copy.start()
        loads.append(copy)

    for field in (base3, cot3):
        for s in range(SAMPLES):
            for plane in range(PLANES + 2):
                low = plane * TRIPLE + CH
                field[s, low : low + CH, 0:SPAN] = jnp.zeros((CH, SPAN), BF16)
                field[s, low : low + CH, PADDED - SPAN : PADDED] = jnp.zeros((CH, SPAN), BF16)
    for at in range(6):
        part[at, :, 0:SPAN] = jnp.zeros((TRIPLE, SPAN), F32)
        part[at, :, PADDED - SPAN : PADDED] = jnp.zeros((TRIPLE, SPAN), F32)

    barrier = pltpu.get_barrier_semaphore()
    peers = [left, right, sibling]
    peers += [xy_peer(at) for at in xy_offsets]
    peers += [z_peer(k) for k in range(1, z_count)]
    for peer in peers:
        pl.semaphore_signal(barrier, inc=1, device_id=peer, device_id_type=MESH)

    eye = (
        lax.broadcasted_iota(jnp.int32, (CH, CH), 0) == lax.broadcasted_iota(jnp.int32, (CH, CH), 1)
    ).astype(BF16)
    loads[0].wait()
    loads[1].wait()
    table = emb[...]
    high = table.astype(BF16)
    rest = table - high.astype(F32)
    middle = rest.astype(BF16)
    low = (rest - middle.astype(F32)).astype(BF16)
    pieces = jnp.concatenate(
        [high.astype(F32), middle.astype(F32), low.astype(F32), jnp.zeros((8, CH), F32)], axis=0
    ).astype(BF16)
    turned = lax.dot_general(eye, pieces, NT, preferred_element_type=F32).astype(BF16)

    def widen(source, s):
        def step(c, carry):
            block = source[s, pl.ds(c * 8, 8)].reshape(8 * PLANES * DEPTH, SPAN)
            wide[s, rows(c * 8 * PLANES * DEPTH, 8 * PLANES * DEPTH), :] = block.astype(F32)
            return carry

        lax.fori_loop(0, CH // 8, step, 0)

    def put(field, s, plane, z, value, order):
        before, after = shifted(value)
        first, last = (after, before) if order > 0 else (before, after)
        low = plane * TRIPLE
        lanes = slice((z + 1) * SPAN, (z + 2) * SPAN)
        field[s, rows(low, CH), lanes] = first.astype(BF16)
        field[s, rows(low + CH, CH), lanes] = value.astype(BF16)
        field[s, rows(low + 2 * CH, CH), lanes] = last.astype(BF16)

    def base_plane(s, x):
        kind = lax.broadcasted_iota(jnp.int32, (32, SPAN), 0) % 8
        for z in range(DEPTH):
            row = labels[s, x, z : z + 1, :]
            hot = (jnp.broadcast_to(row, (32, SPAN)) == kind).astype(F32).astype(BF16)
            looked = jnp.dot(turned, hot, preferred_element_type=F32)
            own = wide[s, pl.ds(x * DEPTH + z, CH, stride=PLANES * DEPTH), :]
            put(base3, s, x + 1, z, own + looked, 1)

    def cot_plane(s, x):
        for z in range(DEPTH):
            own = wide[s, pl.ds(x * DEPTH + z, CH, stride=PLANES * DEPTH), :]
            put(cot3, s, x + 1, z, own, -1)

    def halo(field, which, s):
        inner = slice(SPAN, SPAN + CELLS)
        copies = []
        for side, (at, to, device) in enumerate(
            ((1, PLANES + 1, left), (PLANES, 0, right))
        ):
            copies.append(
                pltpu.make_async_remote_copy(
                    src_ref=field.at[s, at * TRIPLE + CH : at * TRIPLE + 2 * CH, inner],
                    dst_ref=field.at[s, to * TRIPLE + CH : to * TRIPLE + 2 * CH, inner],
                    send_sem=halo_send.at[which, s, side],
                    recv_sem=halo_recv.at[which, s, side],
                    device_id=device,
                    device_id_type=MESH,
                )
            )
        return copies

    def halo_shifts(field, s, order):
        for plane in (0, PLANES + 1):
            low = plane * TRIPLE
            own = field[s, low + CH : low + 2 * CH, SPAN : SPAN + CELLS].astype(F32)
            for z in range(DEPTH):
                lanes = slice((z + 1) * SPAN, (z + 2) * SPAN)
                before, after = shifted(own[:, z * SPAN : (z + 1) * SPAN])
                first, last = (after, before) if order > 0 else (before, after)
                field[s, low : low + CH, lanes] = first.astype(BF16)
                field[s, low + 2 * CH : low + TRIPLE, lanes] = last.astype(BF16)

    halos = [[halo(field, which, s) for s in range(SAMPLES)] for which, field in enumerate((base3, cot3, hid3))]

    for s in range(SAMPLES):
        loads[2 + s].wait()
        widen(feat, s)
        for x in range(PLANES):
            base_plane(s, x)
        if s == 0:
            pl.semaphore_wait(barrier, len(peers))
        for copy in halos[0][s]:
            copy.start()
    for s in range(SAMPLES):
        loads[4 + s].wait()
        widen(cot, s)
        for x in range(PLANES):
            cot_plane(s, x)
        for copy in halos[1][s]:
            copy.start()

    loads[6].wait()
    loads[7].wait()
    def turned_weights(source, target):
        for b in range(3):
            stacked = jnp.concatenate(
                [source[(a * 3 + b) * 3 + e] for a in range(3) for e in range(3)], axis=0
            )
            target[b * CH : (b + 1) * CH, :] = lax.dot_general(
                eye, stacked, NT, preferred_element_type=F32
            ).astype(BF16)

    turned_weights(one, w_one)
    for b in range(3):
        flat = jnp.concatenate(
            [
                lax.dot_general(
                    eye, two[((2 - a) * 3 + b) * 3 + e], NT, preferred_element_type=F32
                ).astype(BF16)
                for a in range(3)
                for e in range(3)
            ],
            axis=0,
        )
        w_back[b * CH : (b + 1) * CH, :] = lax.dot_general(
            eye, flat, NT, preferred_element_type=F32
        ).astype(BF16)
        w_tail[b * CH : (b + 1) * CH, :] = lax.dot_general(
            eye, flat[TRIPLE:], NT, preferred_element_type=F32
        ).astype(BF16)

    def products(field, weights, s, x, at):
        part[at, :, SPAN : SPAN + CELLS] = jnp.dot(
            weights[...],
            field[s, x * TRIPLE : (x + 3) * TRIPLE, SPAN : SPAN + CELLS],
            preferred_element_type=F32,
        )

    def summed(z, order, at):
        total = part[at, CH : 2 * CH, (z + 1) * SPAN : (z + 2) * SPAN]
        total = total + part[at, 0:CH, (z + 1 - order) * SPAN : (z + 2 - order) * SPAN]
        return total + part[at, 2 * CH :, (z + 1 + order) * SPAN : (z + 2 + order) * SPAN]

    def first_layer(s, x, at):
        products(base3, w_one, s, x, at)
        for z in range(DEPTH):
            pre = summed(z, 1, at)
            q = jax.nn.sigmoid(pre)
            factor[s, x, :, z * SPAN : (z + 1) * SPAN] = q * (1.0 + pre * (1.0 - q))
            put(hid3, s, x + 1, z, pre * q, 1)

    def backward_own(s, x, at):
        inner = slice(SPAN, SPAN + CELLS)
        weights, low = (w_tail[...], TRIPLE) if x == 0 else (w_back[:, 0 : 2 * TRIPLE], 3 * TRIPLE)
        part[at, :, inner] = jnp.dot(
            weights, cot3[s, low : low + 2 * TRIPLE, inner], preferred_element_type=F32
        )

    def backward_rest(s, x, at):
        inner = slice(SPAN, SPAN + CELLS)
        weights, low = (w_back[:, 0:TRIPLE], 0) if x == 0 else (w_back[:, 2 * TRIPLE :], 5 * TRIPLE)
        part[at, :, inner] += jnp.dot(
            weights, cot3[s, low : low + TRIPLE, inner], preferred_element_type=F32
        )
        to_d_pre(s, x, at)

    def backward(s, x, at):
        products(cot3, w_back, s, x, at)
        to_d_pre(s, x, at)

    def to_d_pre(s, x, at):
        for z in range(DEPTH):
            d_pre = summed(z, -1, at) * factor[s, x, :, z * SPAN : (z + 1) * SPAN]
            before, after = shifted(d_pre)
            lanes = slice(z * SPAN, (z + 1) * SPAN)
            low = x * TRIPLE
            dpre3[s, low : low + CH, lanes] = before.astype(BF16)
            dpre3[s, low + CH : low + 2 * CH, lanes] = d_pre.astype(BF16)
            dpre3[s, low + 2 * CH : low + TRIPLE, lanes] = after.astype(BF16)

    def second_layer(s, x, at):
        products(hid3, w_two, s, x, at)
        low = (x + 1) * TRIPLE + CH
        for z in range(DEPTH):
            own = base3[s, low : low + CH, (z + 1) * SPAN : (z + 2) * SPAN]
            wide[s, pl.ds(x * DEPTH + z, CH, stride=PLANES * DEPTH), :] = summed(z, 1, at) + own.astype(F32)

    def planes_of(work, places):
        for i, (s, x) in enumerate(places):
            work(s, x, i % 2)

    inner = [(s, x) for s in range(SAMPLES) for x in range(1, PLANES - 1)]
    edges = [(s, x) for s in range(SAMPLES) for x in (0, PLANES - 1)]

    def gradient(a, taps_of, others_of, places):
        taps = jnp.concatenate(
            [
                jnp.concatenate([taps_of(s, x, a, b) for s, x in places], axis=1)
                for b in range(3)
            ],
            axis=0,
        )
        others = jnp.concatenate([others_of(s, x) for s, x in places], axis=1)
        return lax.dot_general(taps, others, NT, preferred_element_type=F32)

    def tap_rows(a):
        return slice(a * TRIPLE, (a + 1) * TRIPLE)

    def base_taps(s, x, a, b):
        low = (x + a) * TRIPLE + CH
        return base3[s, low : low + CH, b * SPAN : b * SPAN + CELLS]

    def d_pre_of(s, x):
        return dpre3[s, x * TRIPLE : (x + 1) * TRIPLE, :]

    def cot_taps(s, x, a, b):
        low = (x + 2 - a) * TRIPLE + CH
        return cot3[s, low : low + CH, (2 - b) * SPAN : (2 - b) * SPAN + CELLS]

    def hidden_of(s, x):
        return hid3[s, (x + 1) * TRIPLE : (x + 2) * TRIPLE, SPAN : SPAN + CELLS]

    def pack(g, total):
        packed[g, 0 : 9 * CH, :] = total[:, 0:SPAN].astype(BF16)
        last = total[:, SPAN:TRIPLE]
        for pair in range(5):
            one_tap = last[2 * pair * CH : (2 * pair + 1) * CH]
            next_tap = last[(2 * pair + 1) * CH : (2 * pair + 2) * CH] if pair < 4 else jnp.zeros_like(one_tap)
            low = (9 + pair) * CH
            packed[g, low : low + CH, :] = jnp.concatenate([one_tap, next_tap], axis=1).astype(BF16)
        packed[g, 14 * CH :, :] = jnp.zeros((PACKED - 14 * CH, SPAN), BF16)

    half = PACKED // 2
    chunk = half // xy_count

    def remote(src, dst, sems, at, peer):
        return pltpu.make_async_remote_copy(
            src_ref=src,
            dst_ref=dst,
            send_sem=sems[0].at[at],
            recv_sem=sems[1].at[at],
            device_id=peer,
            device_id_type=MESH,
        )

    sent = []

    def start(copies):
        for copy in copies:
            copy.start()
        sent.extend(copies)
        return copies

    def arrived(copies):
        for copy in copies:
            copy.wait_recv()

    def my_half():
        return rows(me_core * half, half)

    def my_chunk():
        return rows(me_core * half + me_xy * chunk, chunk)

    def to_sibling(g):
        src = packed.at[g, rows((1 - me_core) * half, half)]
        return start([remote(src, got_core.at[g], sum_core, g, sibling)])

    def spread_xy(g, copies):
        arrived(copies)
        total = packed[g, my_half(), :].astype(F32) + got_core[g].astype(F32)
        mine[g] = total.astype(BF16)
        copies = []
        for k, at in enumerate(xy_offsets):
            src = mine.at[g, rows(xy_index(at) * chunk, chunk)]
            copies.append(remote(src, got_xy.at[g, k], sum_xy, (g, k), xy_peer(at)))
        return start(copies)

    def spread_z(g, copies):
        arrived(copies)
        total = mine[g, rows(me_xy * chunk, chunk), :].astype(F32)
        for k in range(xy_count - 1):
            total = total + got_xy[g, k].astype(F32)
        all_z[g, me_z] = total.astype(BF16)
        own = all_z.at[g, me_z]
        return start([remote(own, own, sum_z, (g, k - 1), z_peer(k)) for k in z_offsets])

    def gather_xy(g, copies):
        arrived(copies)
        total = all_z[g, 0].astype(F32)
        for k in range(1, z_count):
            total = total + all_z[g, k].astype(F32)
        full[g, my_chunk(), :] = (total * scale).astype(BF16)
        own = full.at[g, my_chunk()]
        return start([remote(own, own, back_xy, (g, k), xy_peer(at)) for k, at in enumerate(xy_offsets)])

    def gather_core(g, copies):
        arrived(copies)
        own = full.at[g, my_half()]
        return start([remote(own, own, back_core, g, sibling)])

    def give_back(s):
        def step(c, carry):
            block = wide[s, rows(c * 8 * PLANES * DEPTH, 8 * PLANES * DEPTH), :]
            held[s, pl.ds(c * 8, 8)] = block.reshape(8, PLANES * DEPTH, SPAN).astype(BF16)
            return carry

        lax.fori_loop(0, CH // 8, step, 0)

    planes_of(first_layer, inner)
    planes_of(backward, inner)
    for a in range(3):
        acc[1, tap_rows(a)] = gradient(a, cot_taps, hidden_of, inner)
    for s in range(SAMPLES):
        for copy in halos[0][s]:
            copy.wait_recv()
    for s in range(SAMPLES):
        halo_shifts(base3, s, 1)
    planes_of(first_layer, edges)
    for s in range(SAMPLES):
        for copy in halos[2][s]:
            copy.start()
    for a in range(3):
        acc[0, tap_rows(a)] = gradient(a, base_taps, d_pre_of, inner)
    own_side = ([(s, 0) for s in range(SAMPLES)], edges, [(s, PLANES - 1) for s in range(SAMPLES)])
    for a in range(3):
        acc[1, tap_rows(a)] += gradient(a, cot_taps, hidden_of, own_side[a])
    for i, (s, x) in enumerate(edges):
        backward_own(s, x, 2 + i)
    turned_weights(two, w_two)
    for s in range(SAMPLES):
        for copy in halos[1][s]:
            copy.wait_recv()
    for a in (0, 2):
        acc[1, tap_rows(a)] += gradient(a, cot_taps, hidden_of, own_side[2 - a])
    pack(1, acc[1])
    core_one = to_sibling(1)
    for s in range(SAMPLES):
        halo_shifts(cot3, s, -1)
    for i, (s, x) in enumerate(edges):
        backward_rest(s, x, 2 + i)
    xy_one = spread_xy(1, core_one)
    for a in range(3):
        acc[0, tap_rows(a)] += gradient(a, base_taps, d_pre_of, edges)
    pack(0, acc[0])
    core_zero = to_sibling(0)
    planes_of(second_layer, inner[:2])
    xy_zero = spread_xy(0, core_zero)
    planes_of(second_layer, inner[2:])
    z_one = spread_z(1, xy_one)
    for s in range(SAMPLES):
        for copy in halos[2][s]:
            copy.wait_recv()
    for s in range(SAMPLES):
        halo_shifts(hid3, s, 1)
    planes_of(second_layer, edges)
    z_zero = spread_z(0, xy_zero)
    give_back(0)
    give_back(1)
    full_one = gather_xy(1, z_one)
    full_zero = gather_xy(0, z_zero)
    last_one = gather_core(1, full_one)
    last_zero = gather_core(0, full_zero)
    arrived(last_one)
    arrived(last_zero)

    for field in halos:
        for side in field:
            for copy in side:
                copy.wait_send()
    for copy in sent:
        copy.wait_send()


def finish(held, sums, out_hbm, grad_one, grad_two, spread, sems):
    copies = [pltpu.make_async_copy(held, out_hbm, sems.at[0])]
    copies[0].start()
    eye = (
        lax.broadcasted_iota(jnp.int32, (SPAN, SPAN), 0)
        == lax.broadcasted_iota(jnp.int32, (SPAN, SPAN), 1)
    ).astype(BF16)
    for g, target in enumerate((grad_one, grad_two)):
        for piece in range(14):
            block = sums[g, piece * CH : (piece + 1) * CH, :]
            if g == 0:
                block = block.astype(F32)
                pair = (block[:, 0:CH], block[:, CH:])
            else:
                block = lax.dot_general(eye, block, NT, preferred_element_type=F32)
                pair = (block[0:CH], block[CH:])
            if piece < 9:
                spread[g, piece * 3] = pair[0]
                spread[g, piece * 3 + 1] = pair[1]
            else:
                tap = 2 * (piece - 9)
                spread[g, tap * 3 + 2] = pair[0]
                if tap < 8:
                    spread[g, tap * 3 + 5] = pair[1]
        copies.append(pltpu.make_async_copy(spread.at[g], target, sems.at[1 + g]))
        copies[-1].start()
    for copy in copies:
        copy.wait()


def on_device(dp_count, z_count, features, labels, embedding, weight_one, weight_two, cotangent):
    count = SAMPLES * dp_count * PLANES * z_count * Y_RING * CELLS
    half = PACKED // 2
    xy_count = dp_count // 2 * Y_RING
    chunk = half // xy_count
    flat = (SAMPLES, CH, PLANES * DEPTH, SPAN)
    dma = pltpu.SemaphoreType.DMA
    field = pltpu.VMEM((SAMPLES, (PLANES + 2) * TRIPLE, PADDED), BF16)
    held, sums = pl.pallas_call(
        functools.partial(body, dp_count, z_count, 1.0 / math.sqrt(count)),
        out_shape=(pltpu.VMEM(flat, BF16), pltpu.VMEM((2, PACKED, SPAN), BF16)),
        in_specs=[pl.BlockSpec(memory_space=pltpu.HBM)] * 6,
        out_specs=(pl.BlockSpec(memory_space=pltpu.VMEM),) * 2,
        scratch_shapes=[
            pltpu.VMEM(flat, BF16),
            pltpu.VMEM(flat, BF16),
            pltpu.VMEM((SAMPLES, PLANES, DEPTH, SPAN), jnp.int32),
            pltpu.VMEM((8, CH), F32),
            pltpu.VMEM((27, CH, CH), BF16),
            pltpu.VMEM((27, CH, CH), BF16),
            pltpu.VMEM((SAMPLES, CH * PLANES * DEPTH, SPAN), F32),
            field,
            field,
            field,
            pltpu.VMEM((SAMPLES, PLANES * TRIPLE, CELLS), BF16),
            pltpu.VMEM((SAMPLES, PLANES, CH, CELLS), F32),
            pltpu.VMEM((6, TRIPLE, PADDED), F32),
            pltpu.VMEM((TRIPLE, 3 * TRIPLE), BF16),
            pltpu.VMEM((TRIPLE, 3 * TRIPLE), BF16),
            pltpu.VMEM((TRIPLE, 3 * TRIPLE), BF16),
            pltpu.VMEM((TRIPLE, 2 * TRIPLE), BF16),
            pltpu.VMEM((2, 9 * CH, TRIPLE), F32),
            pltpu.VMEM((2, PACKED, SPAN), BF16),
            pltpu.VMEM((2, half, SPAN), BF16),
            pltpu.VMEM((2, half, SPAN), BF16),
            pltpu.VMEM((2, xy_count - 1, chunk, SPAN), BF16),
            pltpu.VMEM((2, z_count, chunk, SPAN), BF16),
            dma((8,)),
            dma((3, SAMPLES, 2)),
            dma((3, SAMPLES, 2)),
        ]
        + [
            dma(shape)
            for shape in ((2,), (2, xy_count - 1), (2, max(z_count - 1, 1)), (2, xy_count - 1), (2,))
            for _ in range(2)
        ],
        compiler_params=pltpu.CompilerParams(
            collective_id=0, has_side_effects=True, vmem_limit_bytes=56 * 1024 * 1024
        ),
        name="surrogate",
    )(
        features.reshape(flat),
        labels,
        embedding,
        weight_one.reshape(27, CH, CH),
        weight_two.reshape(27, CH, CH),
        cotangent.reshape(flat),
    )
    output, grad_one, grad_two = pl.pallas_call(
        finish,
        out_shape=(
            jax.ShapeDtypeStruct(flat, BF16),
            jax.ShapeDtypeStruct((27, CH, CH), F32),
            jax.ShapeDtypeStruct((27, CH, CH), F32),
        ),
        in_specs=[pl.BlockSpec(memory_space=pltpu.VMEM)] * 2,
        out_specs=(pl.BlockSpec(memory_space=pltpu.HBM),) * 3,
        scratch_shapes=[pltpu.VMEM((2, 27, CH, CH), F32), dma((3,))],
        compiler_params=pltpu.CompilerParams(vmem_limit_bytes=16 * 1024 * 1024),
        name="finish",
    )(held, sums)
    taps = (3, 3, 3, CH, CH)
    return output.reshape(features.shape), grad_one.reshape(taps), grad_two.reshape(taps)


def solution(mesh):
    dp_count = mesh.shape["dp"]
    z_count = mesh.shape["gx"] // Y_RING
    placed = (
        P("dp", None, "gx", None, None),
        P("dp", "gx", None, None),
        P(),
        P(),
        P(),
        P("dp", None, "gx", None, None),
    )
    return jax.shard_map(
        functools.partial(on_device, dp_count, z_count),
        mesh=mesh,
        in_specs=placed,
        out_specs=(P("dp", None, "gx", None, None), P(), P()),
        check_vma=False,
    )
```

```python
import functools
import math

import jax
import jax.numpy as jnp
from jax import lax
from jax.experimental import pallas as pl
from jax.experimental.pallas import tpu as pltpu
from jax.sharding import PartitionSpec as P

MESH = pl.DeviceIdType.MESH
F32 = jnp.float32
BF16 = jnp.bfloat16

CH = 64
PLANES = 4
DEPTH = 8
SPAN = 128
CELLS = DEPTH * SPAN
PADDED = CELLS + 2 * SPAN
TRIPLE = 3 * CH
SAMPLES = 2
PACKED = 1024
Y_RING = 4
NT = (((1,), (1,)), ((), ()))


def rows(start, size, unit=16):
    return pl.ds(pl.multiple_of(start, unit), size)


def shifted(value):
    lane = lax.broadcasted_iota(jnp.int32, value.shape, 1)
    after = jnp.where(lane == 0, 0.0, pltpu.roll(value, 1, 1))
    before = jnp.where(lane == SPAN - 1, 0.0, pltpu.roll(value, SPAN - 1, 1))
    return before, after


def body(
    dp_count,
    z_count,
    scale,
    feat_hbm,
    labels_hbm,
    emb_hbm,
    one_hbm,
    two_hbm,
    cot_hbm,
    held,
    full,
    spread_two,
    feat,
    cot,
    labels,
    emb,
    one,
    two,
    wide,
    base3,
    cot3,
    hid3,
    dpre3,
    factor,
    part,
    w_one,
    w_two,
    w_back,
    w_tail,
    acc,
    packed,
    got_core,
    mine,
    got_xy,
    all_z,
    in_sem,
    halo_send,
    halo_recv,
    *links,
):
    sum_core, sum_xy, sum_z, back_xy, back_core = zip(links[0::2], links[1::2])
    me_dp = lax.axis_index("dp")
    me_gx = lax.axis_index("gx")
    gx_count = z_count * Y_RING
    me_z = me_gx // Y_RING
    me_y = me_gx % Y_RING
    left = (me_dp, (me_gx + gx_count - 1) % gx_count)
    right = (me_dp, (me_gx + 1) % gx_count)

    x_count = dp_count // 2
    me_x = me_dp // 2
    me_core = me_dp % 2
    xy_count = x_count * Y_RING
    me_xy = me_x * Y_RING + me_y
    sibling = (me_x * 2 + 1 - me_core, me_gx)

    def hops(offset, count):
        return min(offset, count - offset)

    xy_offsets = sorted(
        ((dx, dy) for dx in range(x_count) for dy in range(Y_RING) if (dx, dy) != (0, 0)),
        key=lambda at: -(hops(at[0], x_count) + hops(at[1], Y_RING)),
    )
    z_offsets = sorted(range(1, z_count), key=lambda at: -hops(at, z_count))

    def xy_place(at):
        return (me_x + at[0]) % x_count, (me_y + at[1]) % Y_RING

    def xy_peer(at):
        x, y = xy_place(at)
        return (x * 2 + me_core, me_z * Y_RING + y)

    def xy_index(at):
        x, y = xy_place(at)
        return x * Y_RING + y

    def z_peer(k):
        return (me_dp, ((me_z + k) % z_count) * Y_RING + me_y)

    loads = []
    for at, (src, dst) in enumerate(
        (
            (emb_hbm, emb),
            (labels_hbm, labels),
            (feat_hbm.at[0], feat.at[0]),
            (feat_hbm.at[1], feat.at[1]),
            (cot_hbm.at[0], cot.at[0]),
            (cot_hbm.at[1], cot.at[1]),
            (one_hbm, one),
            (two_hbm, two),
        )
    ):
        copy = pltpu.make_async_copy(src, dst, in_sem.at[at])
        copy.start()
        loads.append(copy)

    for field in (base3, cot3):
        for s in range(SAMPLES):
            for plane in range(PLANES + 2):
                low = plane * TRIPLE + CH
                field[s, low : low + CH, 0:SPAN] = jnp.zeros((CH, SPAN), BF16)
                field[s, low : low + CH, PADDED - SPAN : PADDED] = jnp.zeros((CH, SPAN), BF16)
    for at in range(6):
        part[at, :, 0:SPAN] = jnp.zeros((TRIPLE, SPAN), F32)
        part[at, :, PADDED - SPAN : PADDED] = jnp.zeros((TRIPLE, SPAN), F32)

    barrier = pltpu.get_barrier_semaphore()
    peers = [left, right, sibling]
    peers += [xy_peer(at) for at in xy_offsets]
    peers += [z_peer(k) for k in range(1, z_count)]
    for peer in peers:
        pl.semaphore_signal(barrier, inc=1, device_id=peer, device_id_type=MESH)

    eye = (
        lax.broadcasted_iota(jnp.int32, (CH, CH), 0) == lax.broadcasted_iota(jnp.int32, (CH, CH), 1)
    ).astype(BF16)
    loads[0].wait()
    loads[1].wait()
    table = emb[...]
    high = table.astype(BF16)
    rest = table - high.astype(F32)
    middle = rest.astype(BF16)
    low = (rest - middle.astype(F32)).astype(BF16)
    pieces = jnp.concatenate(
        [high.astype(F32), middle.astype(F32), low.astype(F32), jnp.zeros((8, CH), F32)], axis=0
    ).astype(BF16)
    turned = lax.dot_general(eye, pieces, NT, preferred_element_type=F32).astype(BF16)

    def widen(source, s):
        def step(c, carry):
            block = source[s, pl.ds(c * 8, 8)].reshape(8 * PLANES * DEPTH, SPAN)
            wide[s, rows(c * 8 * PLANES * DEPTH, 8 * PLANES * DEPTH), :] = block.astype(F32)
            return carry

        lax.fori_loop(0, CH // 8, step, 0)

    def put(field, s, plane, z, value, order):
        before, after = shifted(value)
        first, last = (after, before) if order > 0 else (before, after)
        low = plane * TRIPLE
        lanes = slice((z + 1) * SPAN, (z + 2) * SPAN)
        field[s, rows(low, CH), lanes] = first.astype(BF16)
        field[s, rows(low + CH, CH), lanes] = value.astype(BF16)
        field[s, rows(low + 2 * CH, CH), lanes] = last.astype(BF16)

    def base_plane(s, x):
        kind = lax.broadcasted_iota(jnp.int32, (32, SPAN), 0) % 8
        for z in range(DEPTH):
            row = labels[s, x, z : z + 1, :]
            hot = (jnp.broadcast_to(row, (32, SPAN)) == kind).astype(F32).astype(BF16)
            looked = jnp.dot(turned, hot, preferred_element_type=F32)
            own = wide[s, pl.ds(x * DEPTH + z, CH, stride=PLANES * DEPTH), :]
            put(base3, s, x + 1, z, own + looked, 1)

    def cot_plane(s, x):
        for z in range(DEPTH):
            own = wide[s, pl.ds(x * DEPTH + z, CH, stride=PLANES * DEPTH), :]
            put(cot3, s, x + 1, z, own, -1)

    def halo(field, which, s):
        inner = slice(SPAN, SPAN + CELLS)
        copies = []
        for side, (at, to, device) in enumerate(
            ((1, PLANES + 1, left), (PLANES, 0, right))
        ):
            copies.append(
                pltpu.make_async_remote_copy(
                    src_ref=field.at[s, at * TRIPLE + CH : at * TRIPLE + 2 * CH, inner],
                    dst_ref=field.at[s, to * TRIPLE + CH : to * TRIPLE + 2 * CH, inner],
                    send_sem=halo_send.at[which, s, side],
                    recv_sem=halo_recv.at[which, s, side],
                    device_id=device,
                    device_id_type=MESH,
                )
            )
        return copies

    def halo_shifts(field, s, order):
        for plane in (0, PLANES + 1):
            low = plane * TRIPLE
            own = field[s, low + CH : low + 2 * CH, SPAN : SPAN + CELLS].astype(F32)
            for z in range(DEPTH):
                lanes = slice((z + 1) * SPAN, (z + 2) * SPAN)
                before, after = shifted(own[:, z * SPAN : (z + 1) * SPAN])
                first, last = (after, before) if order > 0 else (before, after)
                field[s, low : low + CH, lanes] = first.astype(BF16)
                field[s, low + 2 * CH : low + TRIPLE, lanes] = last.astype(BF16)

    halos = [[halo(field, which, s) for s in range(SAMPLES)] for which, field in enumerate((base3, cot3, hid3))]

    for s in range(SAMPLES):
        loads[2 + s].wait()
        widen(feat, s)
        for x in (0, PLANES - 1):
            base_plane(s, x)
        if s == 0:
            pl.semaphore_wait(barrier, len(peers))
        for copy in halos[0][s]:
            copy.start()
    for s in range(SAMPLES):
        for x in range(1, PLANES - 1):
            base_plane(s, x)
    for s in range(SAMPLES):
        loads[4 + s].wait()
        widen(cot, s)

    loads[6].wait()
    loads[7].wait()
    def turned_weights(source, target):
        for b in range(3):
            stacked = jnp.concatenate(
                [source[(a * 3 + b) * 3 + e] for a in range(3) for e in range(3)], axis=0
            )
            target[b * CH : (b + 1) * CH, :] = lax.dot_general(
                eye, stacked, NT, preferred_element_type=F32
            ).astype(BF16)

    turned_weights(one, w_one)
    for b in range(3):
        flat = jnp.concatenate(
            [
                lax.dot_general(
                    eye, two[((2 - a) * 3 + b) * 3 + e], NT, preferred_element_type=F32
                ).astype(BF16)
                for a in range(3)
                for e in range(3)
            ],
            axis=0,
        )
        w_back[b * CH : (b + 1) * CH, :] = lax.dot_general(
            eye, flat, NT, preferred_element_type=F32
        ).astype(BF16)
        w_tail[b * CH : (b + 1) * CH, :] = lax.dot_general(
            eye, flat[TRIPLE:], NT, preferred_element_type=F32
        ).astype(BF16)

    def products(field, weights, s, x, at):
        part[at, :, SPAN : SPAN + CELLS] = jnp.dot(
            weights[...],
            field[s, x * TRIPLE : (x + 3) * TRIPLE, SPAN : SPAN + CELLS],
            preferred_element_type=F32,
        )

    def summed(z, order, at):
        total = part[at, CH : 2 * CH, (z + 1) * SPAN : (z + 2) * SPAN]
        total = total + part[at, 0:CH, (z + 1 - order) * SPAN : (z + 2 - order) * SPAN]
        return total + part[at, 2 * CH :, (z + 1 + order) * SPAN : (z + 2 + order) * SPAN]

    def first_layer(s, x, at):
        products(base3, w_one, s, x, at)
        to_hidden(s, x, at)

    def to_hidden(s, x, at):
        for z in range(DEPTH):
            pre = summed(z, 1, at)
            q = jax.nn.sigmoid(pre)
            factor[s, x, :, z * SPAN : (z + 1) * SPAN] = q * (1.0 + pre * (1.0 - q))
            put(hid3, s, x + 1, z, pre * q, 1)

    def backward_own(s, x, at):
        inner = slice(SPAN, SPAN + CELLS)
        weights, low = (w_tail[...], TRIPLE) if x == 0 else (w_back[:, 0 : 2 * TRIPLE], 3 * TRIPLE)
        part[at, :, inner] = jnp.dot(
            weights, cot3[s, low : low + 2 * TRIPLE, inner], preferred_element_type=F32
        )

    def backward_rest(s, x, at):
        inner = slice(SPAN, SPAN + CELLS)
        weights, low = (w_back[:, 0:TRIPLE], 0) if x == 0 else (w_back[:, 2 * TRIPLE :], 5 * TRIPLE)
        part[at, :, inner] += jnp.dot(
            weights, cot3[s, low : low + TRIPLE, inner], preferred_element_type=F32
        )
        to_d_pre(s, x, at)

    def backward(s, x, at):
        products(cot3, w_back, s, x, at)
        to_d_pre(s, x, at)

    def to_d_pre(s, x, at):
        for z in range(DEPTH):
            d_pre = summed(z, -1, at) * factor[s, x, :, z * SPAN : (z + 1) * SPAN]
            before, after = shifted(d_pre)
            lanes = slice(z * SPAN, (z + 1) * SPAN)
            low = x * TRIPLE
            dpre3[s, low : low + CH, lanes] = before.astype(BF16)
            dpre3[s, low + CH : low + 2 * CH, lanes] = d_pre.astype(BF16)
            dpre3[s, low + 2 * CH : low + TRIPLE, lanes] = after.astype(BF16)

    def second_layer(s, x, at):
        products(hid3, w_two, s, x, at)
        low = (x + 1) * TRIPLE + CH
        for z in range(DEPTH):
            own = base3[s, low : low + CH, (z + 1) * SPAN : (z + 2) * SPAN]
            wide[s, pl.ds(x * DEPTH + z, CH, stride=PLANES * DEPTH), :] = summed(z, 1, at) + own.astype(F32)

    def planes_of(work, places):
        for i, (s, x) in enumerate(places):
            work(s, x, i % 2)

    inner = [(s, x) for s in range(SAMPLES) for x in range(1, PLANES - 1)]
    edges = [(s, x) for s in range(SAMPLES) for x in (0, PLANES - 1)]

    def gradient(a, taps_of, others_of, places):
        taps = jnp.concatenate(
            [
                jnp.concatenate([taps_of(s, x, a, b) for s, x in places], axis=1)
                for b in range(3)
            ],
            axis=0,
        )
        others = jnp.concatenate([others_of(s, x) for s, x in places], axis=1)
        return lax.dot_general(taps, others, NT, preferred_element_type=F32)

    def tap_rows(a):
        return slice(a * TRIPLE, (a + 1) * TRIPLE)

    def base_taps(s, x, a, b):
        low = (x + a) * TRIPLE + CH
        return base3[s, low : low + CH, b * SPAN : b * SPAN + CELLS]

    def d_pre_of(s, x):
        return dpre3[s, x * TRIPLE : (x + 1) * TRIPLE, :]

    def cot_taps(s, x, a, b):
        low = (x + 2 - a) * TRIPLE + CH
        return cot3[s, low : low + CH, (2 - b) * SPAN : (2 - b) * SPAN + CELLS]

    def hidden_of(s, x):
        return hid3[s, (x + 1) * TRIPLE : (x + 2) * TRIPLE, SPAN : SPAN + CELLS]

    def pack(g, total):
        packed[g, 0 : 9 * CH, :] = total[:, 0:SPAN].astype(BF16)
        last = total[:, SPAN:TRIPLE]
        for pair in range(5):
            one_tap = last[2 * pair * CH : (2 * pair + 1) * CH]
            next_tap = last[(2 * pair + 1) * CH : (2 * pair + 2) * CH] if pair < 4 else jnp.zeros_like(one_tap)
            low = (9 + pair) * CH
            packed[g, low : low + CH, :] = jnp.concatenate([one_tap, next_tap], axis=1).astype(BF16)
        packed[g, 14 * CH :, :] = jnp.zeros((PACKED - 14 * CH, SPAN), BF16)

    half = PACKED // 2
    chunk = half // xy_count

    def remote(src, dst, sems, at, peer):
        return pltpu.make_async_remote_copy(
            src_ref=src,
            dst_ref=dst,
            send_sem=sems[0].at[at],
            recv_sem=sems[1].at[at],
            device_id=peer,
            device_id_type=MESH,
        )

    def start(copies):
        for copy in copies:
            copy.start()
        return copies

    def left_device(copies):
        for copy in copies:
            copy.wait_send()

    def arrived(copies):
        for copy in copies:
            copy.wait_recv()

    def my_half():
        return rows(me_core * half, half)

    def my_chunk():
        return rows(me_core * half + me_xy * chunk, chunk)

    def to_sibling(g):
        src = packed.at[g, rows((1 - me_core) * half, half)]
        return start([remote(src, got_core.at[g], sum_core, g, sibling)])

    def spread_xy(g, copies):
        arrived(copies)
        total = packed[g, my_half(), :].astype(F32) + got_core[g].astype(F32)
        mine[g] = total.astype(BF16)
        copies = []
        for k, at in enumerate(xy_offsets):
            src = mine.at[g, rows(xy_index(at) * chunk, chunk)]
            copies.append(remote(src, got_xy.at[g, k], sum_xy, (g, k), xy_peer(at)))
        return start(copies)

    def spread_z(g, copies):
        arrived(copies)
        total = mine[g, rows(me_xy * chunk, chunk), :].astype(F32)
        for k in range(xy_count - 1):
            total = total + got_xy[g, k].astype(F32)
        all_z[g, me_z] = total.astype(BF16)
        own = all_z.at[g, me_z]
        return start([remote(own, own, sum_z, (g, k - 1), z_peer(k)) for k in z_offsets])

    def gather_xy(g, copies):
        arrived(copies)
        total = all_z[g, 0].astype(F32)
        for k in range(1, z_count):
            total = total + all_z[g, k].astype(F32)
        full[g, my_chunk(), :] = (total * scale).astype(BF16)
        own = full.at[g, my_chunk()]
        return start([remote(own, own, back_xy, (g, k), xy_peer(at)) for k, at in enumerate(xy_offsets)])

    def gather_core(g, copies):
        arrived(copies)
        own = full.at[g, my_half()]
        return start([remote(own, own, back_core, g, sibling)])

    def give_back(s):
        def step(c, carry):
            block = wide[s, rows(c * 8 * PLANES * DEPTH, 8 * PLANES * DEPTH), :]
            held[s, pl.ds(c * 8, 8)] = block.reshape(8, PLANES * DEPTH, SPAN).astype(BF16)
            return carry

        lax.fori_loop(0, CH // 8, step, 0)

    for s in range(SAMPLES):
        products(base3, w_one, s, 1, 0)
        cot_plane(s, 0)
        cot_plane(s, PLANES - 1)
        products(base3, w_one, s, 2, 1)
        to_hidden(s, 1, 0)
        cot_plane(s, 1)
        cot_plane(s, 2)
        to_hidden(s, 2, 1)
        for copy in halos[1][s]:
            copy.start()
    planes_of(backward, inner)
    for a in (0, 1):
        acc[1, tap_rows(a)] = gradient(a, cot_taps, hidden_of, inner)
    for s in range(SAMPLES):
        for copy in halos[0][s]:
            copy.wait_recv()
    acc[1, tap_rows(2)] = gradient(2, cot_taps, hidden_of, inner)
    for s in range(SAMPLES):
        halo_shifts(base3, s, 1)
    planes_of(first_layer, edges)
    for s in range(SAMPLES):
        for copy in halos[2][s]:
            copy.start()
    for a in range(3):
        acc[0, tap_rows(a)] = gradient(a, base_taps, d_pre_of, inner)
    own_side = ([(s, 0) for s in range(SAMPLES)], edges, [(s, PLANES - 1) for s in range(SAMPLES)])
    for a in range(3):
        acc[1, tap_rows(a)] += gradient(a, cot_taps, hidden_of, own_side[a])
    for i, (s, x) in enumerate(edges):
        backward_own(s, x, 2 + i)
    turned_weights(two, w_two)
    for s in range(SAMPLES):
        for copy in halos[1][s]:
            copy.wait_recv()
    for a in (0, 2):
        acc[1, tap_rows(a)] += gradient(a, cot_taps, hidden_of, own_side[2 - a])
    for s in range(SAMPLES):
        halo_shifts(cot3, s, -1)
    pack(1, acc[1])
    core_one = to_sibling(1)
    for i, (s, x) in enumerate(edges):
        backward_rest(s, x, 2 + i)
    xy_one = spread_xy(1, core_one)
    for a in range(3):
        acc[0, tap_rows(a)] += gradient(a, base_taps, d_pre_of, edges)
    pack(0, acc[0])
    core_zero = to_sibling(0)
    planes_of(second_layer, inner[:2])
    xy_zero = spread_xy(0, core_zero)
    planes_of(second_layer, inner[2:])
    z_one = spread_z(1, xy_one)
    for s in range(SAMPLES):
        for copy in halos[2][s]:
            copy.wait_recv()
    for s in range(SAMPLES):
        halo_shifts(hid3, s, 1)
    planes_of(second_layer, edges)
    z_zero = spread_z(0, xy_zero)
    give_back(0)
    give_back(1)
    for field in halos:
        for side in field:
            left_device(side)
    left_device(core_one + core_zero + xy_one + xy_zero)
    full_one = gather_xy(1, z_one)
    full_zero = gather_xy(0, z_zero)
    left_device(z_one + z_zero)
    last_one = gather_core(1, full_one)
    left_device(full_one)
    last_zero = gather_core(0, full_zero)
    left_device(full_zero)
    arrived(last_one)
    spread_turned(full, spread_two)
    left_device(last_one)
    arrived(last_zero)
    left_device(last_zero)


def spread_turned(sums, target):
    eye = (
        lax.broadcasted_iota(jnp.int32, (SPAN, SPAN), 0)
        == lax.broadcasted_iota(jnp.int32, (SPAN, SPAN), 1)
    ).astype(BF16)
    for piece in range(14):
        block = sums[1, piece * CH : (piece + 1) * CH, :]
        block = lax.dot_general(eye, block, NT, preferred_element_type=F32)
        if piece < 9:
            target[piece * 3] = block[0:CH]
            target[piece * 3 + 1] = block[CH:]
        else:
            tap = 2 * (piece - 9)
            target[tap * 3 + 2] = block[0:CH]
            if tap < 8:
                target[tap * 3 + 5] = block[CH:]


def finish(held, sums, spread_two, out_hbm, grad_one, grad_two, spread, sems):
    copies = [
        pltpu.make_async_copy(held, out_hbm, sems.at[0]),
        pltpu.make_async_copy(spread_two, grad_two, sems.at[1]),
    ]
    for copy in copies:
        copy.start()
    for piece in range(14):
        block = sums[0, piece * CH : (piece + 1) * CH, :].astype(F32)
        if piece < 9:
            spread[piece * 3] = block[:, 0:CH]
            spread[piece * 3 + 1] = block[:, CH:]
        else:
            tap = 2 * (piece - 9)
            spread[tap * 3 + 2] = block[:, 0:CH]
            if tap < 8:
                spread[tap * 3 + 5] = block[:, CH:]
    copies.append(pltpu.make_async_copy(spread, grad_one, sems.at[2]))
    copies[-1].start()
    for copy in copies:
        copy.wait()


def on_device(dp_count, z_count, features, labels, embedding, weight_one, weight_two, cotangent):
    count = SAMPLES * dp_count * PLANES * z_count * Y_RING * CELLS
    half = PACKED // 2
    xy_count = dp_count // 2 * Y_RING
    chunk = half // xy_count
    flat = (SAMPLES, CH, PLANES * DEPTH, SPAN)
    dma = pltpu.SemaphoreType.DMA
    field = pltpu.VMEM((SAMPLES, (PLANES + 2) * TRIPLE, PADDED), BF16)
    held, sums, spread_two = pl.pallas_call(
        functools.partial(body, dp_count, z_count, 1.0 / math.sqrt(count)),
        out_shape=(
            pltpu.VMEM(flat, BF16),
            pltpu.VMEM((2, PACKED, SPAN), BF16),
            pltpu.VMEM((27, CH, CH), F32),
        ),
        in_specs=[pl.BlockSpec(memory_space=pltpu.HBM)] * 6,
        out_specs=(pl.BlockSpec(memory_space=pltpu.VMEM),) * 3,
        scratch_shapes=[
            pltpu.VMEM(flat, BF16),
            pltpu.VMEM(flat, BF16),
            pltpu.VMEM((SAMPLES, PLANES, DEPTH, SPAN), jnp.int32),
            pltpu.VMEM((8, CH), F32),
            pltpu.VMEM((27, CH, CH), BF16),
            pltpu.VMEM((27, CH, CH), BF16),
            pltpu.VMEM((SAMPLES, CH * PLANES * DEPTH, SPAN), F32),
            field,
            field,
            field,
            pltpu.VMEM((SAMPLES, PLANES * TRIPLE, CELLS), BF16),
            pltpu.VMEM((SAMPLES, PLANES, CH, CELLS), F32),
            pltpu.VMEM((6, TRIPLE, PADDED), F32),
            pltpu.VMEM((TRIPLE, 3 * TRIPLE), BF16),
            pltpu.VMEM((TRIPLE, 3 * TRIPLE), BF16),
            pltpu.VMEM((TRIPLE, 3 * TRIPLE), BF16),
            pltpu.VMEM((TRIPLE, 2 * TRIPLE), BF16),
            pltpu.VMEM((2, 9 * CH, TRIPLE), F32),
            pltpu.VMEM((2, PACKED, SPAN), BF16),
            pltpu.VMEM((2, half, SPAN), BF16),
            pltpu.VMEM((2, half, SPAN), BF16),
            pltpu.VMEM((2, xy_count - 1, chunk, SPAN), BF16),
            pltpu.VMEM((2, z_count, chunk, SPAN), BF16),
            dma((8,)),
            dma((3, SAMPLES, 2)),
            dma((3, SAMPLES, 2)),
        ]
        + [
            dma(shape)
            for shape in ((2,), (2, xy_count - 1), (2, max(z_count - 1, 1)), (2, xy_count - 1), (2,))
            for _ in range(2)
        ],
        compiler_params=pltpu.CompilerParams(
            collective_id=0, has_side_effects=True, vmem_limit_bytes=56 * 1024 * 1024
        ),
        name="surrogate",
    )(
        features.reshape(flat),
        labels,
        embedding,
        weight_one.reshape(27, CH, CH),
        weight_two.reshape(27, CH, CH),
        cotangent.reshape(flat),
    )
    output, grad_one, grad_two = pl.pallas_call(
        finish,
        out_shape=(
            jax.ShapeDtypeStruct(flat, BF16),
            jax.ShapeDtypeStruct((27, CH, CH), F32),
            jax.ShapeDtypeStruct((27, CH, CH), F32),
        ),
        in_specs=[pl.BlockSpec(memory_space=pltpu.VMEM)] * 3,
        out_specs=(pl.BlockSpec(memory_space=pltpu.HBM),) * 3,
        scratch_shapes=[pltpu.VMEM((27, CH, CH), F32), dma((3,))],
        compiler_params=pltpu.CompilerParams(vmem_limit_bytes=16 * 1024 * 1024),
        name="finish",
    )(held, sums, spread_two)
    taps = (3, 3, 3, CH, CH)
    return output.reshape(features.shape), grad_one.reshape(taps), grad_two.reshape(taps)


def solution(mesh):
    dp_count = mesh.shape["dp"]
    z_count = mesh.shape["gx"] // Y_RING
    placed = (
        P("dp", None, "gx", None, None),
        P("dp", "gx", None, None),
        P(),
        P(),
        P(),
        P("dp", None, "gx", None, None),
    )
    return jax.shard_map(
        functools.partial(on_device, dp_count, z_count),
        mesh=mesh,
        in_specs=placed,
        out_specs=(P("dp", None, "gx", None, None), P(), P()),
        check_vma=False,
    )
```
